128 devices in a mesh: dp: 2 (over core), ctx: 16 (over y, x), head: 4 (over z).
Axes of the slice: x: 4, y: 4, z: 4, core: 2. Of those that a mesh axis runs over, the one named last changes fastest.
Arguments:
- queries: bfloat16 [16384, 1024], P(('dp', 'ctx'), 'head'), parts along dimension 0, may hold values from -6 to 6
- keys: bfloat16 [16384, 1024], P(('dp', 'ctx'), 'head'), parts along dimension 0, may hold values from -6 to 6
- values: bfloat16 [16384, 1024], P(('dp', 'ctx'), 'head'), parts along dimension 0, may hold values from -6 to 6
- attn_out: bfloat16 [16384, 1024], P(('dp', 'ctx'), 'head'), parts along dimension 0, may hold values from -6 to 6
- lse: float32 [8, 16384], P('head', ('dp', 'ctx')), parts along dimension 1, may hold values from 3 to 5
- out_grad: bfloat16 [16384, 1024], P(('dp', 'ctx')), parts along dimension 0, may hold values from -6 to 6
- w_out: bfloat16 [1024, 1024], P('head'), may hold values from -0.1875 to 0.1875
- block_utt: int32 [128], P(('dp', 'ctx')), parts along dimension 0, may hold values from 0 to 3, as said below
Outputs:
- grad_q: bfloat16 [16384, 1024], P(('dp', 'ctx'), 'head'), parts along dimension 0
- grad_k: bfloat16 [16384, 1024], P(('dp', 'ctx'), 'head'), parts along dimension 0
- grad_v: bfloat16 [16384, 1024], P(('dp', 'ctx'), 'head'), parts along dimension 0
- grad_w: float32 [1024, 2048], P('ctx', ('dp', 'head')), parts along dimension 1
The draws below stay inside these ranges and needn't reach their ends.
There are 2 independent parts, one for each index of `dp`. The reference program is written for one: setup_inputs(seed, part) draws one part's arguments, and reference() takes and returns one part's arrays. A program takes and returns all parts, laid end to end along the dimension named above; an argument that names none is the same for every part. Nothing has to cross between parts.
Inputs may be any that keep to these rules, and one draw needn't show every extreme that they name: `block_utt`: utterance ids never fall along the pack; each of the 4 utterances holds 1 to 32 blocks, exactly one of them 64 // 2.
All inputs are finite; a program needn't handle non-finite values.
Results may differ from the reference program's by a relative error of at most 0.0066.
Values may be sent and summed in bfloat16 or wider, within the bound.
No kernel may reach another device: no remote copies, remote signals or barrier semaphores. Data moves between devices by JAX's collectives and lax.ppermute only.
A program may use at most 64 MiB of HBM per device.

```python
import jax
import jax.numpy as jnp
from jax import lax

D = 1024
HEADS = 8
HD = 128
BLOCK = 128
NF = 8192
NB = 64


def draw_block_utt(key, part):
    key = jax.random.fold_in(key, 11)
    key_cuts, key_place = jax.random.split(key)
    longest = NB // 2
    remain = NB - longest
    order = jax.random.permutation(key_cuts, remain - 1) + 1
    first = jnp.minimum(order[0], order[1])
    second = jnp.maximum(order[0], order[1])
    others = jnp.stack([first, second - first, remain - second]).astype(jnp.int32)
    place = jax.random.randint(key_place, (), 0, 4)
    slots = jnp.arange(4)
    before = others[jnp.minimum(slots, 2)]
    after = others[jnp.maximum(slots - 1, 0)]
    lengths = jnp.where(slots < place, before, jnp.where(slots == place, jnp.int32(longest), after))
    ends = jnp.cumsum(lengths)[:3]
    blocks = jnp.arange(NB)
    return jnp.sum((blocks[:, None] >= ends[None, :]).astype(jnp.int32), axis=1).astype(jnp.int32)


def spiked(result, rng, source, target, shards_of, factor):
    owner, partner = [(jnp.arange(result.shape[position]) // (result.shape[position] // shards_of)).reshape([-1 if axis == position else 1 for axis in range(result.ndim)]) for position in (source, target)]
    chosen = jax.random.permutation(rng, shards_of)[partner]
    strong = (owner == chosen) | (owner == (partner + shards_of // 2) % shards_of)
    return jnp.where(strong, factor * result, result)


def levels(key, extent, shards, smallest, high):
    factor_of = 1.0
    for position, shards_of in shards:
        steps = jax.random.uniform(jax.random.fold_in(jax.random.fold_in(key, 6), position), (shards_of,), jnp.float32, smallest / len(shards), high / len(shards))
        factor_of = factor_of * jnp.repeat(jnp.exp(steps), extent[position] // shards_of).reshape((-1,) + (1,) * (len(extent) - 1 - position))
    return factor_of


def bell_draw(stream_key, dims, spread, most, pieces=(), held_as=jnp.bfloat16):
    result = spread * jax.random.normal(stream_key, dims, jnp.float32)
    if pieces:
        result = result * levels(stream_key, dims, pieces, -0.22, 0.18)
    return jnp.clip(result, -most, most).astype(held_as)


def bell_draw_with(own_key, dims, width, bound, pieces, heavy, held_as=jnp.bfloat16):
    result = width * jax.random.normal(own_key, dims, jnp.float32)
    if pieces:
        result = result * levels(own_key, dims, pieces, -0.22, 0.18)
    return jnp.clip(spiked(result, jax.random.fold_in(own_key, 3), *heavy), -bound, bound).astype(held_as)


def setup_inputs(seed: int = 0, part: int = 0) -> dict:
    seeds = jax.random.split(jax.random.key(seed), 9)
    part_splits = jax.random.split(jax.random.fold_in(seeds[8], part), 9)
    queries = bell_draw(part_splits[0], (NF, D), 1.0, 6.0, ((0, 16), (1, 4)))
    keys = bell_draw(part_splits[1], (NF, D), 1.0, 6.0, ((0, 16), (1, 4)))
    values = bell_draw(part_splits[2], (NF, D), 1.0, 6.0, ((0, 16), (1, 4)))
    attn_out = bell_draw(part_splits[3], (NF, D), 1.0, 6.0, ((0, 16), (1, 4)))
    lse = jnp.clip(3.0 + 2.0 * jax.random.uniform(part_splits[4], (HEADS, NF), jnp.float32) ** levels(part_splits[4], (HEADS, NF), ((0, 4), (1, 16)), -0.2, 0.2), 3.0, 5.0)
    out_grad = bell_draw_with(part_splits[5], (NF, D), 1.0, 6.0, ((0, 16),), (0, 1, 16, 2.0))
    w_out = bell_draw(seeds[6], (D, D), D ** -0.5, 0.1875, ((0, 4),))
    block_utt = draw_block_utt(jax.random.fold_in(jax.random.fold_in(seeds[8], part), 71), part)
    return {"queries": queries, "keys": keys, "values": values, "attn_out": attn_out, "lse": lse, "out_grad": out_grad, "w_out": w_out, "block_utt": block_utt}


def reference(queries, keys, values, attn_out, lse, out_grad, w_out, block_utt):
    grad_o = lax.dot_general(out_grad, w_out, (((1,), (1,)), ((), ())), preferred_element_type=jnp.float32).astype(jnp.bfloat16)
    grad_w = lax.dot_general(out_grad, attn_out, (((0,), (0,)), ((), ())), preferred_element_type=jnp.float32)
    frames = queries.shape[0]
    query3 = queries.reshape(frames, HEADS, HD).transpose(1, 0, 2)
    key3 = keys.reshape(frames, HEADS, HD).transpose(1, 0, 2)
    value3 = values.reshape(frames, HEADS, HD).transpose(1, 0, 2)
    out3 = attn_out.reshape(frames, HEADS, HD).transpose(1, 0, 2)
    grad3 = grad_o.reshape(frames, HEADS, HD).transpose(1, 0, 2)
    utt = jnp.repeat(block_utt, BLOCK)
    live = utt[:, None] == utt[None, :]
    scale = 1.0 / (HD ** 0.5)

    def one_head(items):
        query, key, value, outs, grads, lse_row = items
        delta = jnp.sum(grads.astype(jnp.float32) * outs.astype(jnp.float32), axis=1)
        scores = jnp.dot(query, key.T, preferred_element_type=jnp.float32) * scale
        prob = jnp.where(live, jnp.exp(scores - lse_row[:, None]), jnp.float32(0.0))
        prob_b = prob.astype(jnp.bfloat16)
        dprob = jnp.dot(grads, value.T, preferred_element_type=jnp.float32)
        dscore = (prob * (dprob - delta[:, None])).astype(jnp.bfloat16)
        dq = (jnp.dot(dscore, key, preferred_element_type=jnp.float32) * scale).astype(jnp.bfloat16)
        dk = (jnp.dot(dscore.T, query, preferred_element_type=jnp.float32) * scale).astype(jnp.bfloat16)
        dv = jnp.dot(prob_b.T, grads, preferred_element_type=jnp.float32).astype(jnp.bfloat16)
        return dq, dk, dv

    dq, dk, dv = lax.map(one_head, (query3, key3, value3, out3, grad3, lse))
    grad_q = dq.transpose(1, 0, 2).reshape(frames, HEADS * HD)
    grad_k = dk.transpose(1, 0, 2).reshape(frames, HEADS * HD)
    grad_v = dv.transpose(1, 0, 2).reshape(frames, HEADS * HD)
    return grad_q, grad_k, grad_v, grad_w
```

```python
import functools
import math

import jax
import jax.numpy as jnp
from jax import lax
from jax.experimental import pallas as pl
from jax.experimental.pallas import tpu as pltpu
from jax.sharding import PartitionSpec as P

SIDE = 4
HD = 128
BLOCK = 128
FRAMES = 512
BLOCKS = FRAMES // BLOCK
EXTRA = 16
GROUP = 4
LOG2E = math.log2(math.e)
SCALE = 1.0 / math.sqrt(HD)
F32 = jnp.float32
BF16 = jnp.bfloat16
NT = (((1,), (1,)), ((), ()))
NN = (((1,), (0,)), ((), ()))
TN = (((0,), (0,)), ((), ()))


def along_x(shard, by):
    pairs = [(y * SIDE + x, y * SIDE + (x + by) % SIDE) for y in range(SIDE) for x in range(SIDE)]
    return lax.ppermute(shard, "ctx", pairs)


def along_y(shard, by):
    pairs = [(y * SIDE + x, ((y + by) % SIDE) * SIDE + x) for y in range(SIDE) for x in range(SIDE)]
    return lax.ppermute(shard, "ctx", pairs)


def dot(a, b, dims):
    return lax.dot_general(a, b, dims, preferred_element_type=F32)


def in_three(row):
    high = row.astype(BF16)
    rest = row - high.astype(F32)
    middle = rest.astype(BF16)
    low = (rest - middle.astype(F32)).astype(BF16)
    return [high, middle, low]


def pack_kernel(q_ref, k_ref, v_ref, o_ref, lse_ref, og_ref, w_ref, x_ref, y_ref):
    grad_o = dot(og_ref[...], w_ref[...], NT).astype(BF16)
    prod = grad_o.astype(F32) * o_ref[...].astype(F32)
    for head, out in ((0, x_ref), (1, y_ref)):
        mine = slice(head * HD, (head + 1) * HD)
        other = slice((1 - head) * HD, (2 - head) * HD)
        out[:FRAMES, 0:HD] = q_ref[:, mine]
        out[:FRAMES, HD:2 * HD] = grad_o[:, mine]
        out[:FRAMES, 2 * HD:3 * HD] = k_ref[:, other]
        out[:FRAMES, 3 * HD:4 * HD] = v_ref[:, other]
        delta = jnp.sum(prod[:, mine].T, axis=0, keepdims=True)
        lse = lse_ref[head:head + 1, :] * F32(LOG2E)
        rows = in_three(lse) + in_three(delta)
        rows.append(jnp.zeros((EXTRA - len(rows), FRAMES), BF16))
        out[FRAMES:, :] = jnp.concatenate(rows, axis=0)


def pack(q, k, v, o, lse, og, w):
    shape = jax.ShapeDtypeStruct((FRAMES + EXTRA, 4 * HD), BF16)
    return pl.pallas_call(
        pack_kernel,
        out_shape=(shape, shape),
        compiler_params=pltpu.CompilerParams(vmem_limit_bytes=32 * 1024 * 1024),
        cost_estimate=pl.CostEstimate(flops=270_000_000, bytes_accessed=4_000_000, transcendentals=0),
    )(q, k, v, o, lse, og, w)


def tiles_kernel(ids_ref, place_ref, *refs):
    xs, ys = refs[0:4], refs[4:8]
    ox, oy = refs[8:12], refs[12:16]
    qd, ks, vs, rows, dk, dv, live = refs[16:]
    y, x = place_ref[0], place_ref[1]
    side = SIDE

    def x_anchor(r):
        return (y * side + lax.rem(x + side - r, side)) * BLOCKS

    def y_anchor(r):
        return (lax.rem(y + side - r, side) * side + x) * BLOCKS

    for r in range(side):
        for head, qsrc, ksrc in ((0, xs[r], ys[r]), (1, ys[r], xs[r])):
            span = pl.ds(r * FRAMES, FRAMES)
            qd[head, span, :] = qsrc[:FRAMES, 0:2 * HD]
            ks[head, span, :] = ksrc[:FRAMES, 2 * HD:3 * HD]
            vs[head, span, :] = ksrc[:FRAMES, 3 * HD:4 * HD]
            extra = qsrc[FRAMES:, :].astype(F32)
            rows[head, r, 0:1, :] = extra[0:1] + extra[1:2] + extra[2:3]
            rows[head, r, 1:2, :] = extra[3:4] + extra[4:5] + extra[5:6]
    dk[...] = jnp.zeros_like(dk)
    dv[...] = jnp.zeros_like(dv)

    def chunk(head, r, q_anchor, k_anchor):
        q_ids = [ids_ref[q_anchor(r) + j] for j in range(BLOCKS)]

        def look(kb, n):
            kid = ids_ref[k_anchor(kb // BLOCKS) + lax.rem(kb, BLOCKS)]
            hit = (kid == q_ids[0]) | (kid == q_ids[1]) | (kid == q_ids[2]) | (kid == q_ids[3])
            live[0, n] = kb
            live[1, n] = kid
            return n + hit.astype(jnp.int32)

        n = lax.fori_loop(0, side * BLOCKS, look, jnp.int32(0))
        for pad in range(GROUP - 1):
            live[0, n + pad] = 0
            live[1, n + pad] = -1
        span = pl.ds(r * FRAMES, FRAMES)
        lane = lax.broadcasted_iota(jnp.int32, (1, FRAMES), 1) // BLOCK
        ids_row = jnp.where(
            lane < 2,
            jnp.where(lane == 0, q_ids[0], q_ids[1]),
            jnp.where(lane == 2, q_ids[2], q_ids[3]),
        )
        lse = rows[head, r, 0:1, :]
        delta = rows[head, r, 1:2, :]

        def unit(g, dq_t):
            query = qd[head, span, 0:HD]
            grad = qd[head, span, HD:2 * HD]
            spans = []
            kids = []
            for j in range(GROUP):
                at = live[0, g * GROUP + j]
                spans.append(pl.ds(pl.multiple_of(at * BLOCK, BLOCK), BLOCK))
                kids.append(live[1, g * GROUP + j])
            key = jnp.concatenate([ks[head, s, :] for s in spans], axis=0)
            value = jnp.concatenate([vs[head, s, :] for s in spans], axis=0)
            scores = dot(key, query, NT)
            dprob = dot(value, grad, NT)
            probs = []
            dscores = []
            for j in range(GROUP):
                cut = slice(j * BLOCK, (j + 1) * BLOCK)
                prob = jnp.exp2(scores[cut] * F32(SCALE * LOG2E) - lse)
                prob = jnp.where(ids_row == kids[j], prob, F32(0.0))
                probs.append(prob.astype(BF16))
                dscores.append((prob * (dprob[cut] - delta)).astype(BF16))
            prob_b = jnp.concatenate(probs, axis=0)
            dscore = jnp.concatenate(dscores, axis=0)
            add_v = dot(prob_b, grad, NN)
            add_k = dot(dscore, query, NN)
            for j in range(GROUP):
                cut = slice(j * BLOCK, (j + 1) * BLOCK)
                dv[head, spans[j], :] += add_v[cut]
                dk[head, spans[j], :] += add_k[cut]
            return dq_t + dot(key, dscore, TN)

        groups = (n + GROUP - 1) // GROUP
        dq_t = lax.fori_loop(0, groups, unit, jnp.zeros((HD, FRAMES), F32))
        return dq_t.T * F32(SCALE)

    for r in range(side):
        dq = chunk(0, r, x_anchor, y_anchor)
        ox[r][:, 0:HD] = dq.astype(ox[r].dtype)
        dq = chunk(1, r, y_anchor, x_anchor)
        oy[r][:, 0:HD] = dq.astype(oy[r].dtype)
    for r in range(side):
        span = pl.ds(r * FRAMES, FRAMES)
        for head, out in ((1, ox[r]), (0, oy[r])):
            out[:, HD:2 * HD] = (dk[head, span, :] * F32(SCALE)).astype(out.dtype)
            out[:, 2 * HD:3 * HD] = dv[head, span, :].astype(out.dtype)


def tiles(ids, place, xs, ys):
    own = jax.ShapeDtypeStruct((FRAMES, 3 * HD), F32)
    sent = jax.ShapeDtypeStruct((FRAMES, 3 * HD), BF16)
    whole = SIDE * FRAMES
    smem = pl.BlockSpec(memory_space=pltpu.SMEM)
    vmem = pl.BlockSpec(memory_space=pltpu.VMEM)
    out = pl.pallas_call(
        tiles_kernel,
        out_shape=(own, sent, sent, sent) * 2,
        in_specs=[smem, smem] + [vmem] * 8,
        out_specs=(vmem,) * 8,
        scratch_shapes=[
            pltpu.VMEM((2, whole, 2 * HD), BF16),
            pltpu.VMEM((2, whole, HD), BF16),
            pltpu.VMEM((2, whole, HD), BF16),
            pltpu.VMEM((2, SIDE, 8, FRAMES), F32),
            pltpu.VMEM((2, whole, HD), F32),
            pltpu.VMEM((2, whole, HD), F32),
            pltpu.SMEM((2, SIDE * BLOCKS + GROUP), jnp.int32),
        ],
        compiler_params=pltpu.CompilerParams(vmem_limit_bytes=56 * 1024 * 1024),
        cost_estimate=pl.CostEstimate(flops=10_000_000_000, bytes_accessed=8_000_000, transcendentals=4_000_000),
    )(ids, place, *xs, *ys)
    return out[0:4], out[4:8]


def merge_kernel(*refs):
    xs, ys = refs[0:4], refs[4:8]
    q_ref, k_ref, v_ref = refs[8:11]
    for out, column, first in ((q_ref, 0, 0), (k_ref, 1, 1), (v_ref, 2, 1)):
        for head in range(2):
            parts = xs if head == first else ys
            cut = slice(column * HD, (column + 1) * HD)
            total = parts[0][:, cut]
            for part in parts[1:]:
                total = total + part[:, cut].astype(F32)
            out[:, head * HD:(head + 1) * HD] = total.astype(BF16)


def merge(xs, ys):
    shape = jax.ShapeDtypeStruct((FRAMES, 2 * HD), BF16)
    return pl.pallas_call(
        merge_kernel,
        out_shape=(shape, shape, shape),
        compiler_params=pltpu.CompilerParams(vmem_limit_bytes=32 * 1024 * 1024),
        cost_estimate=pl.CostEstimate(flops=2_000_000, bytes_accessed=4_000_000, transcendentals=0),
    )(*xs, *ys)


def shards(queries, keys, values, attn_out, lse, out_grad, w_out, block_utt):
    ids = lax.all_gather(block_utt, "ctx", axis=0, tiled=True)
    me = lax.axis_index("ctx")
    place = jnp.stack([me // SIDE, me % SIDE]).astype(jnp.int32)
    px, py = pack(queries, keys, values, attn_out, lse, out_grad, w_out)
    xs = [px, along_x(px, 1), along_x(px, 2), along_x(px, 3)]
    ys = [py, along_y(py, 1), along_y(py, 2), along_y(py, 3)]
    grad_w = lax.psum_scatter(
        lax.dot_general(
            out_grad, attn_out, (((0,), (0,)), ((), ())), preferred_element_type=jnp.float32
        ),
        "ctx",
        scatter_dimension=0,
        tiled=True,
    )
    ox, oy = tiles(ids, place, xs, ys)
    bx = [ox[0]] + [along_x(ox[r], SIDE - r) for r in (1, 2, 3)]
    by = [oy[0]] + [along_y(oy[r], SIDE - r) for r in (1, 2, 3)]
    grad_q, grad_k, grad_v = merge(bx, by)
    return (grad_q, grad_k, grad_v, grad_w)


def solution(mesh):
    return jax.shard_map(
        shards,
        mesh=mesh,
        in_specs=(
            P(("dp", "ctx"), "head"),
            P(("dp", "ctx"), "head"),
            P(("dp", "ctx"), "head"),
            P(("dp", "ctx"), "head"),
            P("head", ("dp", "ctx")),
            P(("dp", "ctx"), None),
            P("head", None),
            P(("dp", "ctx")),
        ),
        out_specs=(
            P(("dp", "ctx"), "head"),
            P(("dp", "ctx"), "head"),
            P(("dp", "ctx"), "head"),
            P("ctx", ("dp", "head")),
        ),
        check_vma=False,
    )
```

```python
import math

import jax
import jax.numpy as jnp
from jax import lax
from jax.experimental import pallas as pl
from jax.experimental.pallas import tpu as pltpu
from jax.sharding import PartitionSpec as P

SIDE = 4
OFFSETS = (0, 1, 3, 2)
EARLY = 3
HD = 128
BLOCK = 128
FRAMES = 512
BLOCKS = FRAMES // BLOCK
WIDTH = 1024
EXTRA = 16
GROUP = 4
LOG2E = math.log2(math.e)
SCALE = 1.0 / math.sqrt(HD)
F32 = jnp.float32
BF16 = jnp.bfloat16
NT = (((1,), (1,)), ((), ()))
NN = (((1,), (0,)), ((), ()))
TN = (((0,), (0,)), ((), ()))
ANY = pl.BlockSpec(memory_space=pl.ANY)
VMEM = pl.BlockSpec(memory_space=pltpu.VMEM)
SMEM = pl.BlockSpec(memory_space=pltpu.SMEM)
GW_ROWS = WIDTH // SIDE
GW_OWN = WIDTH // SIDE // SIDE
MIB = 1024 * 1024


def along_x(shard, by):
    pairs = [(y * SIDE + x, y * SIDE + (x + by) % SIDE) for y in range(SIDE) for x in range(SIDE)]
    return lax.ppermute(shard, "ctx", pairs)


def along_y(shard, by):
    pairs = [(y * SIDE + x, ((y + by) % SIDE) * SIDE + x) for y in range(SIDE) for x in range(SIDE)]
    return lax.ppermute(shard, "ctx", pairs)


def dot(a, b, dims):
    return lax.dot_general(a, b, dims, preferred_element_type=F32)


def in_three(row):
    high = row.astype(BF16)
    rest = row - high.astype(F32)
    middle = rest.astype(BF16)
    low = (rest - middle.astype(F32)).astype(BF16)
    return [high, middle, low]


def fetch(pairs, sem):
    copies = [pltpu.make_async_copy(a, b, sem.at[i]) for i, (a, b) in enumerate(pairs)]
    for copy in copies:
        copy.start()
    return copies


def pack_kernel(ids_ref, lse_ref, og_hbm, w_hbm, o_hbm, q_hbm, k_hbm, v_hbm, x_ref, y_ref, og, w, o, sem):
    ins = [(og_hbm, og), (w_hbm, w), (o_hbm, o)]
    rows = pl.ds(0, FRAMES)
    for head, out in ((0, x_ref), (1, y_ref)):
        mine = pl.ds(head * HD, HD)
        other = pl.ds((1 - head) * HD, HD)
        ins.append((q_hbm.at[:, mine], out.at[rows, pl.ds(0, HD)]))
        ins.append((k_hbm.at[:, other], out.at[rows, pl.ds(2 * HD, HD)]))
        ins.append((v_hbm.at[:, other], out.at[rows, pl.ds(3 * HD, HD)]))
    copies = fetch(ins, sem)
    lane = lax.broadcasted_iota(jnp.int32, (1, FRAMES), 1) // BLOCK
    ids = jnp.where(
        lane < 2,
        jnp.where(lane == 0, ids_ref[0], ids_ref[1]),
        jnp.where(lane == 2, ids_ref[2], ids_ref[3]),
    ).astype(F32).astype(BF16)
    copies[0].wait()
    copies[1].wait()
    grad_o = dot(og[...], w[...], NT).astype(BF16)
    copies[2].wait()
    prod = grad_o.astype(F32) * o[...].astype(F32)
    for head, out in ((0, x_ref), (1, y_ref)):
        mine = slice(head * HD, (head + 1) * HD)
        out[:FRAMES, HD:2 * HD] = grad_o[:, mine]
        delta = jnp.sum(prod[:, mine].T, axis=0, keepdims=True)
        lse = lse_ref[head:head + 1, :] * F32(LOG2E)
        extra = in_three(lse) + in_three(delta) + [ids]
        extra.append(jnp.zeros((EXTRA - len(extra), FRAMES), BF16))
        out[FRAMES:, :] = jnp.concatenate(extra, axis=0)
    for copy in copies[3:]:
        copy.wait()


def pack(q, k, v, o, lse, og, w, ids):
    shape = jax.ShapeDtypeStruct((FRAMES + EXTRA, 4 * HD), BF16)
    return pl.pallas_call(
        pack_kernel,
        out_shape=(shape, shape),
        in_specs=[SMEM, VMEM] + [ANY] * 6,
        out_specs=(VMEM, VMEM),
        scratch_shapes=[
            pltpu.VMEM((FRAMES, WIDTH), BF16),
            pltpu.VMEM((2 * HD, WIDTH), BF16),
            pltpu.VMEM((FRAMES, 2 * HD), BF16),
            pltpu.SemaphoreType.DMA((9,)),
        ],
        compiler_params=pltpu.CompilerParams(vmem_limit_bytes=56 * MIB),
        cost_estimate=pl.CostEstimate(flops=270_000_000, bytes_accessed=4_000_000, transcendentals=0),
    )(ids, lse, og, w, o, q, k, v)


def weight_kernel(og_hbm, o_hbm, own_ref, one_ref, two_ref, three_ref, og, o, sem):
    copies = fetch([(og_hbm, og), (o_hbm, o)], sem)
    for copy in copies:
        copy.wait()
    for r, out in enumerate((own_ref, one_ref, two_ref, three_ref)):
        at = lax.rem(lax.axis_index("ctx") // SIDE + r, SIDE) * GW_ROWS
        part = og[:, pl.ds(pl.multiple_of(at, GW_ROWS), GW_ROWS)]
        out[...] = dot(part, o[...], TN).astype(out.dtype)


def weight(og, o):
    own = jax.ShapeDtypeStruct((GW_ROWS, 2 * HD), F32)
    sent = jax.ShapeDtypeStruct((GW_ROWS, 2 * HD), BF16)
    return pl.pallas_call(
        weight_kernel,
        out_shape=(own, sent, sent, sent),
        in_specs=[ANY, ANY],
        out_specs=(VMEM,) * 4,
        scratch_shapes=[
            pltpu.VMEM((FRAMES, WIDTH), BF16),
            pltpu.VMEM((FRAMES, 2 * HD), BF16),
            pltpu.SemaphoreType.DMA((2,)),
        ],
        compiler_params=pltpu.CompilerParams(vmem_limit_bytes=40 * MIB),
        cost_estimate=pl.CostEstimate(flops=270_000_000, bytes_accessed=3_000_000, transcendentals=0),
    )(og, o)


def load_chunks(slots, xs, ys, qd, ks, vs, extras, rows, ids_v, ids_s, sem, id_sem):
    copies = []
    for s in range(slots):
        span = pl.ds(s * FRAMES, FRAMES)
        top = pl.ds(0, FRAMES)
        bottom = pl.ds(FRAMES, EXTRA)
        for head, qsrc, ksrc in ((0, xs[s], ys[s]), (1, ys[s], xs[s])):
            copies += fetch(
                [
                    (qsrc.at[bottom, :], extras.at[head, s]),
                    (qsrc.at[top, pl.ds(0, 2 * HD)], qd.at[head, span]),
                    (ksrc.at[top, pl.ds(2 * HD, HD)], ks.at[head, span]),
                    (ksrc.at[top, pl.ds(3 * HD, HD)], vs.at[head, span]),
                ],
                sem.at[2 * s + head],
            )
    for copy in copies[0::4]:
        copy.wait()
    for s in range(slots):
        for head in range(2):
            extra = extras[head, s].astype(F32)
            rows[head, s, 0:1, :] = extra[0:1] + extra[1:2] + extra[2:3]
            rows[head, s, 1:2, :] = extra[3:4] + extra[4:5] + extra[5:6]
            rows[head, s, 2:3, :] = extra[6:7]
            ids_v[head * SIDE + s:head * SIDE + s + 1, :] = extra[6:7].astype(jnp.int32)
    to_scalars = pltpu.make_async_copy(ids_v, ids_s, id_sem)
    to_scalars.start()
    return copies, to_scalars


def run_chunk(head, s, k_slots, dq_t, qd, ks, vs, rows, ids_s, live, dk, dv):
    q_row, k_row = head * SIDE, (1 - head) * SIDE
    q_ids = [ids_s[q_row + s, j * BLOCK] for j in range(BLOCKS)]
    n = jnp.int32(0)
    for ks_slot in k_slots:
        for j in range(BLOCKS):
            kid = ids_s[k_row + ks_slot, j * BLOCK]
            hit = (kid == q_ids[0]) | (kid == q_ids[1]) | (kid == q_ids[2]) | (kid == q_ids[3])
            live[0, n] = ks_slot * BLOCKS + j
            live[1, n] = kid
            n = n + hit.astype(jnp.int32)
    for pad in range(GROUP - 1):
        live[0, n + pad] = k_slots[0] * BLOCKS
        live[1, n + pad] = -1
    span = pl.ds(s * FRAMES, FRAMES)
    lse = rows[head, s, 0:1, :]
    delta = rows[head, s, 1:2, :]
    ids_row = rows[head, s, 2:3, :].astype(jnp.int32)

    def unit(g, total):
        query = qd[head, span, 0:HD]
        grad = qd[head, span, HD:2 * HD]
        spans = []
        kids = []
        for j in range(GROUP):
            at = live[0, g * GROUP + j]
            spans.append(pl.ds(pl.multiple_of(at * BLOCK, BLOCK), BLOCK))
            kids.append(live[1, g * GROUP + j])
        key = jnp.concatenate([ks[head, p, :] for p in spans], axis=0)
        value = jnp.concatenate([vs[head, p, :] for p in spans], axis=0)
        scores = dot(key, query, NT)
        dprob = dot(value, grad, NT)
        probs = []
        dscores = []
        for j in range(GROUP):
            cut = slice(j * BLOCK, (j + 1) * BLOCK)
            prob = jnp.exp2(scores[cut] * F32(SCALE * LOG2E) - lse)
            prob = jnp.where(ids_row == kids[j], prob, F32(0.0))
            probs.append(prob.astype(BF16))
            dscores.append((prob * (dprob[cut] - delta)).astype(BF16))
        prob_b = jnp.concatenate(probs, axis=0)
        dscore = jnp.concatenate(dscores, axis=0)
        add_v = dot(prob_b, grad, NN)
        add_k = dot(dscore, query, NN)
        for j in range(GROUP):
            cut = slice(j * BLOCK, (j + 1) * BLOCK)
            dv[head, spans[j], :] += add_v[cut]
            dk[head, spans[j], :] += add_k[cut]
        return total + dot(key, dscore, TN)

    groups = (n + GROUP - 1) // GROUP
    return lax.fori_loop(0, groups, unit, dq_t)


def early_kernel(*refs):
    xs, ys = refs[0:EARLY], refs[EARLY:2 * EARLY]
    dk, dv, dq_t = refs[2 * EARLY:2 * EARLY + 3]
    qd, ks, vs, extras, rows, ids_v, ids_s, live, sem, id_sem = refs[2 * EARLY + 3:]
    copies, to_scalars = load_chunks(EARLY, xs, ys, qd, ks, vs, extras, rows, ids_v, ids_s, sem, id_sem)
    dk[...] = jnp.zeros_like(dk)
    dv[...] = jnp.zeros_like(dv)
    to_scalars.wait()
    for i, copy in enumerate(copies):
        if i % 4:
            copy.wait()
    zero = jnp.zeros((HD, FRAMES), F32)
    for s in range(EARLY):
        for head in range(2):
            dq_t[head, s] = run_chunk(head, s, range(EARLY), zero, qd, ks, vs, rows, ids_s, live, dk, dv)


def late_kernel(*refs):
    xs, ys = refs[0:4], refs[4:8]
    old_k, old_v, old_q = refs[8:11]
    gw = refs[11:15]
    ox, oy = refs[15:19], refs[19:23]
    dk, dv, gw_sum, qd, ks, vs, extras, rows, ids_v, ids_s, live, sem, id_sem = refs[23:]
    copies, to_scalars = load_chunks(SIDE, xs, ys, qd, ks, vs, extras, rows, ids_v, ids_s, sem, id_sem)
    done = EARLY * FRAMES
    dk[:, 0:done, :] = old_k[...]
    dv[:, 0:done, :] = old_v[...]
    dk[:, done:, :] = jnp.zeros_like(dk[:, done:, :])
    dv[:, done:, :] = jnp.zeros_like(dv[:, done:, :])
    total = gw[0][...]
    for part in gw[1:]:
        total = total + part[...].astype(F32)
    gw_sum[...] = total
    for s in range(SIDE):
        at = lax.rem(lax.axis_index("ctx") + SIDE - OFFSETS[s], SIDE) * GW_OWN
        piece = gw_sum[pl.ds(pl.multiple_of(at, GW_OWN), GW_OWN), :]
        ox[s][FRAMES:, 0:2 * HD] = piece.astype(ox[s].dtype)
        ox[s][FRAMES:, 2 * HD:] = jnp.zeros((GW_OWN, HD), ox[s].dtype)
    to_scalars.wait()
    for i, copy in enumerate(copies):
        if i % 4:
            copy.wait()
    for s in range(SIDE):
        for head, out in ((0, ox[s]), (1, oy[s])):
            early = s < EARLY
            start = old_q[head, s] if early else jnp.zeros((HD, FRAMES), F32)
            k_slots = range(EARLY, SIDE) if early else range(SIDE)
            dq_t = run_chunk(head, s, k_slots, start, qd, ks, vs, rows, ids_s, live, dk, dv)
            out[:FRAMES, 0:HD] = (dq_t.T * F32(SCALE)).astype(out.dtype)
    for s in range(SIDE):
        span = pl.ds(s * FRAMES, FRAMES)
        for head, out in ((1, ox[s]), (0, oy[s])):
            out[:FRAMES, HD:2 * HD] = (dk[head, span, :] * F32(SCALE)).astype(out.dtype)
            out[:FRAMES, 2 * HD:3 * HD] = dv[head, span, :].astype(out.dtype)


def chunk_scratch(slots):
    whole = slots * FRAMES
    return [
        pltpu.VMEM((2, whole, 2 * HD), BF16),
        pltpu.VMEM((2, whole, HD), BF16),
        pltpu.VMEM((2, whole, HD), BF16),
        pltpu.VMEM((2, slots, EXTRA, FRAMES), BF16),
        pltpu.VMEM((2, slots, 8, FRAMES), F32),
        pltpu.VMEM((2 * SIDE, FRAMES), jnp.int32),
        pltpu.SMEM((2 * SIDE, FRAMES), jnp.int32),
        pltpu.SMEM((2, SIDE * BLOCKS + GROUP), jnp.int32),
        pltpu.SemaphoreType.DMA((2 * slots, 4)),
        pltpu.SemaphoreType.DMA,
    ]


def early_tiles(xs, ys):
    kv = jax.ShapeDtypeStruct((2, EARLY * FRAMES, HD), F32)
    q = jax.ShapeDtypeStruct((2, EARLY, HD, FRAMES), F32)
    return pl.pallas_call(
        early_kernel,
        out_shape=(kv, kv, q),
        in_specs=[ANY] * (2 * EARLY),
        out_specs=(VMEM,) * 3,
        scratch_shapes=chunk_scratch(EARLY),
        compiler_params=pltpu.CompilerParams(vmem_limit_bytes=40 * MIB),
        cost_estimate=pl.CostEstimate(flops=5_000_000_000, bytes_accessed=8_000_000, transcendentals=2_000_000),
    )(*xs, *ys)


def late_tiles(xs, ys, partial, gw):
    rows_x, rows_y = FRAMES + GW_OWN, FRAMES
    shapes = [
        jax.ShapeDtypeStruct((rows, 3 * HD), F32 if s == 0 else BF16) for rows in (rows_x, rows_y) for s in range(SIDE)
    ]
    acc = pltpu.VMEM((2, SIDE * FRAMES, HD), F32)
    out = pl.pallas_call(
        late_kernel,
        out_shape=tuple(shapes),
        in_specs=[ANY] * 8 + [VMEM] * 7,
        out_specs=(VMEM,) * 8,
        scratch_shapes=[acc, acc, pltpu.VMEM((GW_ROWS, 2 * HD), F32)] + chunk_scratch(SIDE),
        compiler_params=pltpu.CompilerParams(vmem_limit_bytes=40 * MIB),
        cost_estimate=pl.CostEstimate(flops=5_000_000_000, bytes_accessed=8_000_000, transcendentals=2_000_000),
    )(*xs, *ys, *partial, *gw)
    return out[0:4], out[4:8]


def merge_kernel(*refs):
    xs, ys = refs[0:4], refs[4:8]
    q_ref, k_ref, v_ref, w_ref = refs[8:12]
    for out, column, first in ((q_ref, 0, 0), (k_ref, 1, 1), (v_ref, 2, 1)):
        for head in range(2):
            parts = xs if head == first else ys
            cut = slice(column * HD, (column + 1) * HD)
            total = parts[0][:FRAMES, cut]
            for part in parts[1:]:
                total = total + part[:FRAMES, cut].astype(F32)
            out[:, head * HD:(head + 1) * HD] = total.astype(BF16)
    total = xs[0][FRAMES:, 0:2 * HD]
    for part in xs[1:]:
        total = total + part[FRAMES:, 0:2 * HD].astype(F32)
    w_ref[...] = total


def merge(xs, ys):
    shape = jax.ShapeDtypeStruct((FRAMES, 2 * HD), BF16)
    return pl.pallas_call(
        merge_kernel,
        out_shape=(shape, shape, shape, jax.ShapeDtypeStruct((GW_OWN, 2 * HD), F32)),
        compiler_params=pltpu.CompilerParams(vmem_limit_bytes=32 * MIB),
        cost_estimate=pl.CostEstimate(flops=2_000_000, bytes_accessed=4_000_000, transcendentals=0),
    )(*xs, *ys)


def shards(queries, keys, values, attn_out, lse, out_grad, w_out, block_utt):
    px, py = pack(queries, keys, values, attn_out, lse, out_grad, w_out, block_utt)
    xs = [px] + [along_x(px, by) for by in OFFSETS[1:]]
    ys = [py] + [along_y(py, by) for by in OFFSETS[1:]]
    gw = weight(out_grad, attn_out)
    gw = [gw[0]] + [along_y(gw[r], r) for r in (1, 2, 3)]
    partial = early_tiles(xs[:EARLY], ys[:EARLY])
    ox, oy = late_tiles(xs, ys, partial, gw)
    bx = [ox[0]] + [along_x(ox[s], SIDE - OFFSETS[s]) for s in (1, 2, 3)]
    by = [oy[0]] + [along_y(oy[s], SIDE - OFFSETS[s]) for s in (1, 2, 3)]
    return merge(bx, by)


def solution(mesh):
    return jax.shard_map(
        shards,
        mesh=mesh,
        in_specs=(
            P(("dp", "ctx"), "head"),
            P(("dp", "ctx"), "head"),
            P(("dp", "ctx"), "head"),
            P(("dp", "ctx"), "head"),
            P("head", ("dp", "ctx")),
            P(("dp", "ctx"), None),
            P("head", None),
            P(("dp", "ctx")),
        ),
        out_specs=(
            P(("dp", "ctx"), "head"),
            P(("dp", "ctx"), "head"),
            P(("dp", "ctx"), "head"),
            P("ctx", ("dp", "head")),
        ),
        check_vma=False,
    )
```

```python
import math

import jax
import jax.numpy as jnp
from jax import lax
from jax.experimental import pallas as pl
from jax.experimental.pallas import tpu as pltpu
from jax.sharding import PartitionSpec as P

SIDE = 4
OFFSETS = (0, 1, 3, 2)
EARLY = 3
HD = 128
BLOCK = 128
FRAMES = 512
BLOCKS = FRAMES // BLOCK
WIDTH = 1024
EXTRA = 16
GROUP = 4
LOG2E = math.log2(math.e)
SCALE = 1.0 / math.sqrt(HD)
F32 = jnp.float32
BF16 = jnp.bfloat16
NT = (((1,), (1,)), ((), ()))
NN = (((1,), (0,)), ((), ()))
TN = (((0,), (0,)), ((), ()))
ANY = pl.BlockSpec(memory_space=pl.ANY)
VMEM = pl.BlockSpec(memory_space=pltpu.VMEM)
SMEM = pl.BlockSpec(memory_space=pltpu.SMEM)
GW_ROWS = WIDTH // SIDE
GW_OWN = WIDTH // SIDE // SIDE
MIB = 1024 * 1024


def along_x(shard, by):
    pairs = [(y * SIDE + x, y * SIDE + (x + by) % SIDE) for y in range(SIDE) for x in range(SIDE)]
    return lax.ppermute(shard, "ctx", pairs)


def along_y(shard, by):
    pairs = [(y * SIDE + x, ((y + by) % SIDE) * SIDE + x) for y in range(SIDE) for x in range(SIDE)]
    return lax.ppermute(shard, "ctx", pairs)


def dot(a, b, dims):
    return lax.dot_general(a, b, dims, preferred_element_type=F32)


def in_three(row):
    high = row.astype(BF16)
    rest = row - high.astype(F32)
    middle = rest.astype(BF16)
    low = (rest - middle.astype(F32)).astype(BF16)
    return [high, middle, low]


def fetch(pairs, sem):
    copies = [pltpu.make_async_copy(a, b, sem.at[i]) for i, (a, b) in enumerate(pairs)]
    for copy in copies:
        copy.start()
    return copies


def pack_kernel(ids_ref, lse_ref, og_hbm, w_hbm, o_hbm, q_hbm, k_hbm, v_hbm, x_ref, y_ref, og, w, o, sem):
    ins = [(og_hbm, og), (w_hbm, w), (o_hbm, o)]
    rows = pl.ds(0, FRAMES)
    for head, out in ((0, x_ref), (1, y_ref)):
        mine = pl.ds(head * HD, HD)
        other = pl.ds((1 - head) * HD, HD)
        ins.append((q_hbm.at[:, mine], out.at[rows, pl.ds(0, HD)]))
        ins.append((k_hbm.at[:, other], out.at[rows, pl.ds(2 * HD, HD)]))
        ins.append((v_hbm.at[:, other], out.at[rows, pl.ds(3 * HD, HD)]))
    copies = fetch(ins, sem)
    lane = lax.broadcasted_iota(jnp.int32, (1, FRAMES), 1) // BLOCK
    ids = jnp.where(
        lane < 2,
        jnp.where(lane == 0, ids_ref[0], ids_ref[1]),
        jnp.where(lane == 2, ids_ref[2], ids_ref[3]),
    ).astype(F32).astype(BF16)
    copies[0].wait()
    copies[1].wait()
    grad_o = dot(og[...], w[...], NT).astype(BF16)
    copies[2].wait()
    prod = grad_o.astype(F32) * o[...].astype(F32)
    for head, out in ((0, x_ref), (1, y_ref)):
        mine = slice(head * HD, (head + 1) * HD)
        out[:FRAMES, HD:2 * HD] = grad_o[:, mine]
        delta = jnp.sum(prod[:, mine].T, axis=0, keepdims=True)
        lse = lse_ref[head:head + 1, :] * F32(LOG2E)
        extra = in_three(lse) + in_three(delta) + [ids]
        extra.append(jnp.zeros((EXTRA - len(extra), FRAMES), BF16))
        out[FRAMES:, :] = jnp.concatenate(extra, axis=0)
    for copy in copies[3:]:
        copy.wait()


def pack(q, k, v, o, lse, og, w, ids):
    shape = jax.ShapeDtypeStruct((FRAMES + EXTRA, 4 * HD), BF16)
    return pl.pallas_call(
        pack_kernel,
        out_shape=(shape, shape),
        in_specs=[SMEM, VMEM] + [ANY] * 6,
        out_specs=(VMEM, VMEM),
        scratch_shapes=[
            pltpu.VMEM((FRAMES, WIDTH), BF16),
            pltpu.VMEM((2 * HD, WIDTH), BF16),
            pltpu.VMEM((FRAMES, 2 * HD), BF16),
            pltpu.SemaphoreType.DMA((9,)),
        ],
        compiler_params=pltpu.CompilerParams(vmem_limit_bytes=56 * MIB),
        cost_estimate=pl.CostEstimate(flops=270_000_000, bytes_accessed=4_000_000, transcendentals=0),
    )(ids, lse, og, w, o, q, k, v)


def weight_kernel(og_hbm, o_hbm, px, py, own_ref, one_ref, two_ref, three_ref, hx, hy, og, o, sem):
    copies = fetch([(og_hbm, og), (o_hbm, o), (px, hx), (py, hy)], sem)
    copies[0].wait()
    copies[1].wait()
    for r, out in enumerate((own_ref, one_ref, two_ref, three_ref)):
        at = lax.rem(lax.axis_index("ctx") // SIDE + r, SIDE) * GW_ROWS
        part = og[:, pl.ds(pl.multiple_of(at, GW_ROWS), GW_ROWS)]
        out[...] = dot(part, o[...], TN).astype(out.dtype)
    copies[2].wait()
    copies[3].wait()


def weight(og, o, px, py):
    own = jax.ShapeDtypeStruct((GW_ROWS, 2 * HD), F32)
    sent = jax.ShapeDtypeStruct((GW_ROWS, 2 * HD), BF16)
    held = jax.ShapeDtypeStruct(px.shape, BF16)
    return pl.pallas_call(
        weight_kernel,
        out_shape=(own, sent, sent, sent, held, held),
        in_specs=[ANY] * 4,
        out_specs=(VMEM,) * 6,
        scratch_shapes=[
            pltpu.VMEM((FRAMES, WIDTH), BF16),
            pltpu.VMEM((FRAMES, 2 * HD), BF16),
            pltpu.SemaphoreType.DMA((4,)),
        ],
        compiler_params=pltpu.CompilerParams(vmem_limit_bytes=40 * MIB),
        cost_estimate=pl.CostEstimate(flops=270_000_000, bytes_accessed=3_000_000, transcendentals=0),
    )(og, o, px, py)


def load_chunks(slots, xs, ys, qd, ks, vs, extras, rows, ids_v, ids_s, sem, id_sem):
    copies = []
    for s in range(slots):
        span = pl.ds(s * FRAMES, FRAMES)
        top = pl.ds(0, FRAMES)
        bottom = pl.ds(FRAMES, EXTRA)
        for head, qsrc, ksrc in ((0, xs[s], ys[s]), (1, ys[s], xs[s])):
            copies += fetch(
                [
                    (qsrc.at[bottom, :], extras.at[head, s]),
                    (qsrc.at[top, pl.ds(0, 2 * HD)], qd.at[head, span]),
                    (ksrc.at[top, pl.ds(2 * HD, HD)], ks.at[head, span]),
                    (ksrc.at[top, pl.ds(3 * HD, HD)], vs.at[head, span]),
                ],
                sem.at[2 * s + head],
            )
    for copy in copies[0::4]:
        copy.wait()
    for s in range(slots):
        for head in range(2):
            extra = extras[head, s].astype(F32)
            rows[head, s, 0:1, :] = extra[0:1] + extra[1:2] + extra[2:3]
            rows[head, s, 1:2, :] = extra[3:4] + extra[4:5] + extra[5:6]
            rows[head, s, 2:3, :] = extra[6:7]
            ids_v[head * SIDE + s:head * SIDE + s + 1, :] = extra[6:7].astype(jnp.int32)
    to_scalars = pltpu.make_async_copy(ids_v, ids_s, id_sem)
    to_scalars.start()
    return copies, to_scalars


def run_chunk(head, s, k_slots, dq_t, qd, ks, vs, rows, ids_s, live, dk, dv):
    q_row, k_row = head * SIDE, (1 - head) * SIDE
    q_ids = [ids_s[q_row + s, j * BLOCK] for j in range(BLOCKS)]
    n = jnp.int32(0)
    for ks_slot in k_slots:
        for j in range(BLOCKS):
            kid = ids_s[k_row + ks_slot, j * BLOCK]
            hit = (kid == q_ids[0]) | (kid == q_ids[1]) | (kid == q_ids[2]) | (kid == q_ids[3])
            live[0, n] = ks_slot * BLOCKS + j
            live[1, n] = kid
            n = n + hit.astype(jnp.int32)
    for pad in range(GROUP - 1):
        live[0, n + pad] = k_slots[0] * BLOCKS
        live[1, n + pad] = -1
    span = pl.ds(s * FRAMES, FRAMES)
    lse = rows[head, s, 0:1, :]
    delta = rows[head, s, 1:2, :]
    ids_row = rows[head, s, 2:3, :].astype(jnp.int32)

    def unit(g, total):
        query = qd[head, span, 0:HD]
        grad = qd[head, span, HD:2 * HD]
        spans = []
        kids = []
        for j in range(GROUP):
            at = live[0, g * GROUP + j]
            spans.append(pl.ds(pl.multiple_of(at * BLOCK, BLOCK), BLOCK))
            kids.append(live[1, g * GROUP + j])
        key = jnp.concatenate([ks[head, p, :] for p in spans], axis=0)
        value = jnp.concatenate([vs[head, p, :] for p in spans], axis=0)
        half = FRAMES // 2
        cuts = [slice(0, half), slice(half, FRAMES)]
        fronts = [(dot(key, query[c], NT), dot(value, grad[c], NT)) for c in cuts]
        add_v = add_k = None
        add_q = []
        for c, (scores, dprob) in zip(cuts, fronts):
            probs = []
            dscores = []
            for j in range(GROUP):
                cut = slice(j * BLOCK, (j + 1) * BLOCK)
                prob = jnp.exp2(scores[cut] * F32(SCALE * LOG2E) - lse[:, c])
                prob = jnp.where(ids_row[:, c] == kids[j], prob, F32(0.0))
                probs.append(prob.astype(BF16))
                dscores.append((prob * (dprob[cut] - delta[:, c])).astype(BF16))
            prob_b = jnp.concatenate(probs, axis=0)
            dscore = jnp.concatenate(dscores, axis=0)
            part_v = dot(prob_b, grad[c], NN)
            part_k = dot(dscore, query[c], NN)
            add_v = part_v if add_v is None else add_v + part_v
            add_k = part_k if add_k is None else add_k + part_k
            add_q.append(dot(key, dscore, TN))
        for j in range(GROUP):
            cut = slice(j * BLOCK, (j + 1) * BLOCK)
            dv[head, spans[j], :] += add_v[cut]
            dk[head, spans[j], :] += add_k[cut]
        return total + jnp.concatenate(add_q, axis=1)

    groups = (n + GROUP - 1) // GROUP
    return lax.fori_loop(0, groups, unit, dq_t)


def early_kernel(*refs):
    xs, ys = refs[0:EARLY], refs[EARLY:2 * EARLY]
    dk, dv, dq_t = refs[2 * EARLY:2 * EARLY + 3]
    qd, ks, vs, extras, rows, ids_v, ids_s, live, sem, id_sem = refs[2 * EARLY + 3:]
    copies, to_scalars = load_chunks(EARLY, xs, ys, qd, ks, vs, extras, rows, ids_v, ids_s, sem, id_sem)
    dk[...] = jnp.zeros_like(dk)
    dv[...] = jnp.zeros_like(dv)
    to_scalars.wait()
    for i, copy in enumerate(copies):
        if i % 4:
            copy.wait()
    zero = jnp.zeros((HD, FRAMES), F32)
    for s in range(EARLY):
        for head in range(2):
            dq_t[head, s] = run_chunk(head, s, range(EARLY), zero, qd, ks, vs, rows, ids_s, live, dk, dv)


def late_kernel(*refs):
    xs, ys = refs[0:4], refs[4:8]
    old_k, old_v, old_q = refs[8:11]
    gw = refs[11:15]
    ox, oy = refs[15:19], refs[19:23]
    dk, dv, gw_sum, qd, ks, vs, extras, rows, ids_v, ids_s, live, sem, id_sem = refs[23:]
    copies, to_scalars = load_chunks(SIDE, xs, ys, qd, ks, vs, extras, rows, ids_v, ids_s, sem, id_sem)
    done = EARLY * FRAMES
    dk[:, 0:done, :] = old_k[...]
    dv[:, 0:done, :] = old_v[...]
    dk[:, done:, :] = jnp.zeros_like(dk[:, done:, :])
    dv[:, done:, :] = jnp.zeros_like(dv[:, done:, :])
    total = gw[0][...]
    for part in gw[1:]:
        total = total + part[...].astype(F32)
    gw_sum[...] = total
    for s in range(SIDE):
        at = lax.rem(lax.axis_index("ctx") + SIDE - OFFSETS[s], SIDE) * GW_OWN
        piece = gw_sum[pl.ds(pl.multiple_of(at, GW_OWN), GW_OWN), :]
        ox[s][FRAMES:, 0:2 * HD] = piece.astype(ox[s].dtype)
        ox[s][FRAMES:, 2 * HD:] = jnp.zeros((GW_OWN, HD), ox[s].dtype)
    to_scalars.wait()
    for i, copy in enumerate(copies):
        if i % 4:
            copy.wait()
    for s in range(SIDE):
        for head, out in ((0, ox[s]), (1, oy[s])):
            early = s < EARLY
            start = old_q[head, s] if early else jnp.zeros((HD, FRAMES), F32)
            k_slots = range(EARLY, SIDE) if early else range(SIDE)
            dq_t = run_chunk(head, s, k_slots, start, qd, ks, vs, rows, ids_s, live, dk, dv)
            out[:FRAMES, 0:HD] = (dq_t.T * F32(SCALE)).astype(out.dtype)
    for s in range(SIDE):
        span = pl.ds(s * FRAMES, FRAMES)
        for head, out in ((1, ox[s]), (0, oy[s])):
            out[:FRAMES, HD:2 * HD] = (dk[head, span, :] * F32(SCALE)).astype(out.dtype)
            out[:FRAMES, 2 * HD:3 * HD] = dv[head, span, :].astype(out.dtype)


def chunk_scratch(slots):
    whole = slots * FRAMES
    return [
        pltpu.VMEM((2, whole, 2 * HD), BF16),
        pltpu.VMEM((2, whole, HD), BF16),
        pltpu.VMEM((2, whole, HD), BF16),
        pltpu.VMEM((2, slots, EXTRA, FRAMES), BF16),
        pltpu.VMEM((2, slots, 8, FRAMES), F32),
        pltpu.VMEM((2 * SIDE, FRAMES), jnp.int32),
        pltpu.SMEM((2 * SIDE, FRAMES), jnp.int32),
        pltpu.SMEM((2, SIDE * BLOCKS + GROUP), jnp.int32),
        pltpu.SemaphoreType.DMA((2 * slots, 4)),
        pltpu.SemaphoreType.DMA,
    ]


def early_tiles(xs, ys):
    kv = jax.ShapeDtypeStruct((2, EARLY * FRAMES, HD), F32)
    q = jax.ShapeDtypeStruct((2, EARLY, HD, FRAMES), F32)
    return pl.pallas_call(
        early_kernel,
        out_shape=(kv, kv, q),
        in_specs=[ANY] * (2 * EARLY),
        out_specs=(VMEM,) * 3,
        scratch_shapes=chunk_scratch(EARLY),
        compiler_params=pltpu.CompilerParams(vmem_limit_bytes=40 * MIB),
        cost_estimate=pl.CostEstimate(flops=5_000_000_000, bytes_accessed=8_000_000, transcendentals=2_000_000),
    )(*xs, *ys)


def late_tiles(xs, ys, partial, gw):
    rows_x, rows_y = FRAMES + GW_OWN, FRAMES
    shapes = [
        jax.ShapeDtypeStruct((rows, 3 * HD), F32 if s == 0 else BF16) for rows in (rows_x, rows_y) for s in range(SIDE)
    ]
    acc = pltpu.VMEM((2, SIDE * FRAMES, HD), F32)
    out = pl.pallas_call(
        late_kernel,
        out_shape=tuple(shapes),
        in_specs=[ANY] * 8 + [VMEM] * 7,
        out_specs=(VMEM,) * 8,
        scratch_shapes=[acc, acc, pltpu.VMEM((GW_ROWS, 2 * HD), F32)] + chunk_scratch(SIDE),
        compiler_params=pltpu.CompilerParams(vmem_limit_bytes=40 * MIB),
        cost_estimate=pl.CostEstimate(flops=5_000_000_000, bytes_accessed=8_000_000, transcendentals=2_000_000),
    )(*xs, *ys, *partial, *gw)
    return out[0:4], out[4:8]


def merge_kernel(*refs):
    xs, ys = refs[0:4], refs[4:8]
    q_ref, k_ref, v_ref, w_ref = refs[8:12]
    for out, column, first in ((q_ref, 0, 0), (k_ref, 1, 1), (v_ref, 2, 1)):
        for head in range(2):
            parts = xs if head == first else ys
            cut = slice(column * HD, (column + 1) * HD)
            total = parts[0][:FRAMES, cut]
            for part in parts[1:]:
                total = total + part[:FRAMES, cut].astype(F32)
            out[:, head * HD:(head + 1) * HD] = total.astype(BF16)
    total = xs[0][FRAMES:, 0:2 * HD]
    for part in xs[1:]:
        total = total + part[FRAMES:, 0:2 * HD].astype(F32)
    w_ref[...] = total


def merge(xs, ys):
    shape = jax.ShapeDtypeStruct((FRAMES, 2 * HD), BF16)
    return pl.pallas_call(
        merge_kernel,
        out_shape=(shape, shape, shape, jax.ShapeDtypeStruct((GW_OWN, 2 * HD), F32)),
        compiler_params=pltpu.CompilerParams(vmem_limit_bytes=32 * MIB),
        cost_estimate=pl.CostEstimate(flops=2_000_000, bytes_accessed=4_000_000, transcendentals=0),
    )(*xs, *ys)


def shards(queries, keys, values, attn_out, lse, out_grad, w_out, block_utt):
    px, py = pack(queries, keys, values, attn_out, lse, out_grad, w_out, block_utt)
    near = [along_x(px, 1), along_y(py, 1), along_x(px, 3), along_y(py, 3)]
    *gw, held_x, held_y = weight(out_grad, attn_out, px, py)
    gw = [gw[0]] + [along_y(gw[r], r) for r in (1, 2, 3)]
    px, py, held_x, held_y, *near = lax.optimization_barrier((px, py, held_x, held_y, *near))
    xs = [held_x, near[0], near[2], along_x(px, 2)]
    ys = [held_y, near[1], near[3], along_y(py, 2)]
    partial = early_tiles(xs[:EARLY], ys[:EARLY])
    ox, oy = late_tiles(xs, ys, partial, gw)
    bx = [ox[0]] + [along_x(ox[s], SIDE - OFFSETS[s]) for s in (1, 2, 3)]
    by = [oy[0]] + [along_y(oy[s], SIDE - OFFSETS[s]) for s in (1, 2, 3)]
    return merge(bx, by)


def solution(mesh):
    return jax.shard_map(
        shards,
        mesh=mesh,
        in_specs=(
            P(("dp", "ctx"), "head"),
            P(("dp", "ctx"), "head"),
            P(("dp", "ctx"), "head"),
            P(("dp", "ctx"), "head"),
            P("head", ("dp", "ctx")),
            P(("dp", "ctx"), None),
            P("head", None),
            P(("dp", "ctx")),
        ),
        out_specs=(
            P(("dp", "ctx"), "head"),
            P(("dp", "ctx"), "head"),
            P(("dp", "ctx"), "head"),
            P("ctx", ("dp", "head")),
        ),
        check_vma=False,
    )
```

```python
import math

import jax
import jax.numpy as jnp
from jax import lax
from jax.experimental import pallas as pl
from jax.experimental.pallas import tpu as pltpu
from jax.sharding import PartitionSpec as P

SIDE = 4
OFFSETS = (0, 1, 3, 2)
EARLY = 3
HD = 128
BLOCK = 128
FRAMES = 512
BLOCKS = FRAMES // BLOCK
WIDTH = 1024
EXTRA = 16
GROUP = 4
LOG2E = math.log2(math.e)
SCALE = 1.0 / math.sqrt(HD)
F32 = jnp.float32
BF16 = jnp.bfloat16
NT = (((1,), (1,)), ((), ()))
NN = (((1,), (0,)), ((), ()))
TN = (((0,), (0,)), ((), ()))
ANY = pl.BlockSpec(memory_space=pl.ANY)
VMEM = pl.BlockSpec(memory_space=pltpu.VMEM)
SMEM = pl.BlockSpec(memory_space=pltpu.SMEM)
GW = WIDTH // SIDE // SIDE
GW_OUT = GW // 2
MIB = 1024 * 1024


def along_x(shard, by):
    pairs = [(y * SIDE + x, y * SIDE + (x + by) % SIDE) for y in range(SIDE) for x in range(SIDE)]
    return lax.ppermute(shard, "ctx", pairs)


def along_y(shard, by):
    pairs = [(y * SIDE + x, ((y + by) % SIDE) * SIDE + x) for y in range(SIDE) for x in range(SIDE)]
    return lax.ppermute(shard, "ctx", pairs)


def dot(a, b, dims):
    return lax.dot_general(a, b, dims, preferred_element_type=F32)


def in_three(row):
    high = row.astype(BF16)
    rest = row - high.astype(F32)
    middle = rest.astype(BF16)
    low = (rest - middle.astype(F32)).astype(BF16)
    return [high, middle, low]


def fetch(pairs, sem):
    copies = [pltpu.make_async_copy(a, b, sem.at[i]) for i, (a, b) in enumerate(pairs)]
    for copy in copies:
        copy.start()
    return copies


def pack_kernel(ids_ref, lse_ref, og_hbm, w_hbm, o_hbm, q_hbm, k_hbm, v_hbm, *refs):
    own = refs[0:2]
    sent = (refs[2:5], refs[5:8])
    og, w, o, whole, body, low, sem, out_sem = refs[8:]
    ins = [(og_hbm, og), (w_hbm, w), (o_hbm, o)]
    rows = pl.ds(0, FRAMES)
    for head in range(2):
        mine = pl.ds(head * HD, HD)
        other = pl.ds((1 - head) * HD, HD)
        ins.append((q_hbm.at[:, mine], body.at[head, rows, pl.ds(0, HD)]))
        ins.append((k_hbm.at[:, other], body.at[head, rows, pl.ds(2 * HD, HD)]))
        ins.append((v_hbm.at[:, other], body.at[head, rows, pl.ds(3 * HD, HD)]))
    copies = fetch(ins, sem)
    lane = lax.broadcasted_iota(jnp.int32, (1, FRAMES), 1) // BLOCK
    ids = jnp.where(
        lane < 2,
        jnp.where(lane == 0, ids_ref[0], ids_ref[1]),
        jnp.where(lane == 2, ids_ref[2], ids_ref[3]),
    ).astype(F32).astype(BF16)
    copies[0].wait()
    copies[1].wait()
    grad_o = dot(og[...], w[...], NT).astype(BF16)
    copies[2].wait()
    prod = grad_o.astype(F32) * o[...].astype(F32)
    for copy in copies[3:]:
        copy.wait()
    outs = []
    top, bottom = pl.ds(0, FRAMES + EXTRA), pl.ds(FRAMES + EXTRA, GW)
    for head in range(2):
        mine = slice(head * HD, (head + 1) * HD)
        body[head, :FRAMES, HD:2 * HD] = grad_o[:, mine]
        delta = jnp.sum(prod[:, mine].T, axis=0, keepdims=True)
        lse = lse_ref[head:head + 1, :] * F32(LOG2E)
        extra = in_three(lse) + in_three(delta) + [ids]
        extra.append(jnp.zeros((EXTRA - len(extra), FRAMES), BF16))
        body[head, FRAMES:, :] = jnp.concatenate(extra, axis=0)
        outs += fetch([(body.at[head], out.at[top]) for out in sent[head]], out_sem.at[head])
    whole[...] = dot(og[...], o[...], TN)
    me = (lax.rem(lax.axis_index("ctx"), SIDE), lax.axis_index("ctx") // SIDE)
    for i in range(2):
        for n, r in enumerate((0,) + OFFSETS[1:]):
            to = lax.rem(me[i] + r, SIDE)
            for part in range(SIDE):
                at = (part * SIDE + to if i == 0 else to * SIDE + part) * GW
                piece = whole[pl.ds(pl.multiple_of(at, GW), GW), (1 - i) * HD:(2 - i) * HD]
                cut = slice(part * HD, (part + 1) * HD)
                if n == 0:
                    own[i][:, cut] = piece
                else:
                    low[i, n - 1, :, cut] = piece.astype(BF16)
        outs += fetch([(low.at[i, n], out.at[bottom]) for n, out in enumerate(sent[i])], out_sem.at[2 + i])
    for copy in outs:
        copy.wait()


def pack(q, k, v, o, lse, og, w, ids):
    sent = jax.ShapeDtypeStruct((FRAMES + EXTRA + GW, 4 * HD), BF16)
    own = jax.ShapeDtypeStruct((GW, 4 * HD), F32)
    out = pl.pallas_call(
        pack_kernel,
        out_shape=(own, own) + (sent,) * 6,
        in_specs=[SMEM, VMEM] + [ANY] * 6,
        out_specs=(VMEM, VMEM) + (ANY,) * 6,
        scratch_shapes=[
            pltpu.VMEM((FRAMES, WIDTH), BF16),
            pltpu.VMEM((2 * HD, WIDTH), BF16),
            pltpu.VMEM((FRAMES, 2 * HD), BF16),
            pltpu.VMEM((WIDTH, 2 * HD), F32),
            pltpu.VMEM((2, FRAMES + EXTRA, 4 * HD), BF16),
            pltpu.VMEM((2, SIDE - 1, GW, 4 * HD), BF16),
            pltpu.SemaphoreType.DMA((9,)),
            pltpu.SemaphoreType.DMA((4, SIDE - 1)),
        ],
        compiler_params=pltpu.CompilerParams(vmem_limit_bytes=58 * MIB),
        cost_estimate=pl.CostEstimate(flops=540_000_000, bytes_accessed=6_000_000, transcendentals=0),
    )(ids, lse, og, w, o, q, k, v)
    return out[0], out[1], out[2:5], out[5:8]


def hold_kernel(px, py, hx, hy, sem):
    top = pl.ds(0, FRAMES + EXTRA)
    for copy in fetch([(px.at[top], hx), (py.at[top], hy)], sem):
        copy.wait()


def hold(px, py):
    shape = jax.ShapeDtypeStruct((FRAMES + EXTRA, 4 * HD), BF16)
    return pl.pallas_call(
        hold_kernel,
        out_shape=(shape, shape),
        in_specs=[ANY] * 2,
        out_specs=(VMEM,) * 2,
        scratch_shapes=[pltpu.SemaphoreType.DMA((2,))],
        compiler_params=pltpu.CompilerParams(vmem_limit_bytes=40 * MIB),
        cost_estimate=pl.CostEstimate(flops=0, bytes_accessed=2_000_000, transcendentals=0),
    )(px, py)


def load_chunks(slots, xs, ys, qd, ks, vs, extras, rows, ids_v, ids_s, sem, id_sem):
    copies = []
    for s in range(slots):
        span = pl.ds(s * FRAMES, FRAMES)
        top = pl.ds(0, FRAMES)
        bottom = pl.ds(FRAMES, EXTRA)
        for head, qsrc, ksrc in ((0, xs[s], ys[s]), (1, ys[s], xs[s])):
            copies += fetch(
                [
                    (qsrc.at[bottom, :], extras.at[head, s]),
                    (qsrc.at[top, pl.ds(0, 2 * HD)], qd.at[head, span]),
                    (ksrc.at[top, pl.ds(2 * HD, HD)], ks.at[head, span]),
                    (ksrc.at[top, pl.ds(3 * HD, HD)], vs.at[head, span]),
                ],
                sem.at[2 * s + head],
            )
    for copy in copies[0::4]:
        copy.wait()
    for s in range(slots):
        for head in range(2):
            extra = extras[head, s].astype(F32)
            rows[head, s, 0:1, :] = extra[0:1] + extra[1:2] + extra[2:3]
            rows[head, s, 1:2, :] = extra[3:4] + extra[4:5] + extra[5:6]
            rows[head, s, 2:3, :] = extra[6:7]
            ids_v[head * SIDE + s:head * SIDE + s + 1, :] = extra[6:7].astype(jnp.int32)
    to_scalars = pltpu.make_async_copy(ids_v, ids_s, id_sem)
    to_scalars.start()
    return copies, to_scalars


def run_chunk(head, s, k_slots, dq_t, qd, ks, vs, rows, ids_s, live, dk, dv):
    q_row, k_row = head * SIDE, (1 - head) * SIDE
    q_ids = [ids_s[q_row + s, j * BLOCK] for j in range(BLOCKS)]
    n = jnp.int32(0)
    for ks_slot in k_slots:
        for j in range(BLOCKS):
            kid = ids_s[k_row + ks_slot, j * BLOCK]
            hit = (kid == q_ids[0]) | (kid == q_ids[1]) | (kid == q_ids[2]) | (kid == q_ids[3])
            live[0, n] = ks_slot * BLOCKS + j
            live[1, n] = kid
            n = n + hit.astype(jnp.int32)
    for pad in range(GROUP - 1):
        live[0, n + pad] = k_slots[0] * BLOCKS
        live[1, n + pad] = -1
    span = pl.ds(s * FRAMES, FRAMES)
    lse = rows[head, s, 0:1, :]
    delta = rows[head, s, 1:2, :]
    ids_row = rows[head, s, 2:3, :].astype(jnp.int32)

    def unit(g, total):
        query = qd[head, span, 0:HD]
        grad = qd[head, span, HD:2 * HD]
        spans = []
        kids = []
        for j in range(GROUP):
            at = live[0, g * GROUP + j]
            spans.append(pl.ds(pl.multiple_of(at * BLOCK, BLOCK), BLOCK))
            kids.append(live[1, g * GROUP + j])
        key = jnp.concatenate([ks[head, p, :] for p in spans], axis=0)
        value = jnp.concatenate([vs[head, p, :] for p in spans], axis=0)
        half = FRAMES // 2
        cuts = [slice(0, half), slice(half, FRAMES)]
        fronts = [(dot(key, query[c], NT), dot(value, grad[c], NT)) for c in cuts]
        add_v = add_k = None
        add_q = []
        for c, (scores, dprob) in zip(cuts, fronts):
            probs = []
            dscores = []
            for j in range(GROUP):
                cut = slice(j * BLOCK, (j + 1) * BLOCK)
                prob = jnp.exp2(scores[cut] * F32(SCALE * LOG2E) - lse[:, c])
                prob = jnp.where(ids_row[:, c] == kids[j], prob, F32(0.0))
                probs.append(prob.astype(BF16))
                dscores.append((prob * (dprob[cut] - delta[:, c])).astype(BF16))
            prob_b = jnp.concatenate(probs, axis=0)
            dscore = jnp.concatenate(dscores, axis=0)
            part_v = dot(prob_b, grad[c], NN)
            part_k = dot(dscore, query[c], NN)
            add_v = part_v if add_v is None else add_v + part_v
            add_k = part_k if add_k is None else add_k + part_k
            add_q.append(dot(key, dscore, TN))
        for j in range(GROUP):
            cut = slice(j * BLOCK, (j + 1) * BLOCK)
            dv[head, spans[j], :] += add_v[cut]
            dk[head, spans[j], :] += add_k[cut]
        return total + jnp.concatenate(add_q, axis=1)

    groups = (n + GROUP - 1) // GROUP
    return lax.fori_loop(0, groups, unit, dq_t)


def early_kernel(*refs):
    xs, ys = refs[0:EARLY], refs[EARLY:2 * EARLY]
    dk, dv, dq_t = refs[2 * EARLY:2 * EARLY + 3]
    qd, ks, vs, extras, rows, ids_v, ids_s, live, sem, id_sem = refs[2 * EARLY + 3:]
    copies, to_scalars = load_chunks(EARLY, xs, ys, qd, ks, vs, extras, rows, ids_v, ids_s, sem, id_sem)
    dk[...] = jnp.zeros_like(dk)
    dv[...] = jnp.zeros_like(dv)
    to_scalars.wait()
    for i, copy in enumerate(copies):
        if i % 4:
            copy.wait()
    zero = jnp.zeros((HD, FRAMES), F32)
    for s in range(EARLY):
        for head in range(2):
            dq_t[head, s] = run_chunk(head, s, range(EARLY), zero, qd, ks, vs, rows, ids_s, live, dk, dv)


def late_kernel(*refs):
    xs, ys = refs[0:4], refs[4:8]
    old_k, old_v, old_q = refs[8:11]
    gw_own = refs[11:13]
    ox, oy = refs[13:17], refs[17:21]
    dk, dv, gw_in, gw_sum, gw_sem, qd, ks, vs, extras, rows, ids_v, ids_s, live, sem, id_sem = refs[21:]
    low = pl.ds(FRAMES + EXTRA, GW)
    gw_copies = []
    for i, parts in enumerate((xs, ys)):
        gw_copies += fetch([(part.at[low], gw_in.at[i, n]) for n, part in enumerate(parts[1:])], gw_sem.at[i])
    copies, to_scalars = load_chunks(SIDE, xs, ys, qd, ks, vs, extras, rows, ids_v, ids_s, sem, id_sem)
    done = EARLY * FRAMES
    dk[:, 0:done, :] = old_k[...]
    dv[:, 0:done, :] = old_v[...]
    dk[:, done:, :] = jnp.zeros_like(dk[:, done:, :])
    dv[:, done:, :] = jnp.zeros_like(dv[:, done:, :])
    me = (lax.rem(lax.axis_index("ctx"), SIDE), lax.axis_index("ctx") // SIDE)
    for copy in gw_copies:
        copy.wait()
    for i in range(2):
        total = gw_own[i][...]
        for n in range(SIDE - 1):
            total = total + gw_in[i, n].astype(F32)
        gw_sum[i] = total
    for s in range(SIDE):
        for i, out in ((1, ox[s]), (0, oy[s])):
            at = lax.rem(me[1 - i] + SIDE - OFFSETS[s], SIDE) * HD
            cut = pl.ds(pl.multiple_of(at, HD), HD)
            out[FRAMES:, 0:HD] = gw_sum[i, 0:GW_OUT, cut].astype(out.dtype)
            out[FRAMES:, HD:2 * HD] = gw_sum[i, GW_OUT:GW, cut].astype(out.dtype)
            out[FRAMES:, 2 * HD:] = jnp.zeros((GW_OUT, HD), out.dtype)
    to_scalars.wait()
    for i, copy in enumerate(copies):
        if i % 4:
            copy.wait()
    for s in range(SIDE):
        for head, out in ((0, ox[s]), (1, oy[s])):
            early = s < EARLY
            start = old_q[head, s] if early else jnp.zeros((HD, FRAMES), F32)
            k_slots = range(EARLY, SIDE) if early else range(SIDE)
            dq_t = run_chunk(head, s, k_slots, start, qd, ks, vs, rows, ids_s, live, dk, dv)
            out[:FRAMES, 0:HD] = (dq_t.T * F32(SCALE)).astype(out.dtype)
    for s in range(SIDE):
        span = pl.ds(s * FRAMES, FRAMES)
        for head, out in ((1, ox[s]), (0, oy[s])):
            out[:FRAMES, HD:2 * HD] = (dk[head, span, :] * F32(SCALE)).astype(out.dtype)
            out[:FRAMES, 2 * HD:3 * HD] = dv[head, span, :].astype(out.dtype)


def chunk_scratch(slots):
    whole = slots * FRAMES
    return [
        pltpu.VMEM((2, whole, 2 * HD), BF16),
        pltpu.VMEM((2, whole, HD), BF16),
        pltpu.VMEM((2, whole, HD), BF16),
        pltpu.VMEM((2, slots, EXTRA, FRAMES), BF16),
        pltpu.VMEM((2, slots, 8, FRAMES), F32),
        pltpu.VMEM((2 * SIDE, FRAMES), jnp.int32),
        pltpu.SMEM((2 * SIDE, FRAMES), jnp.int32),
        pltpu.SMEM((2, SIDE * BLOCKS + GROUP), jnp.int32),
        pltpu.SemaphoreType.DMA((2 * slots, 4)),
        pltpu.SemaphoreType.DMA,
    ]


def early_tiles(xs, ys):
    kv = jax.ShapeDtypeStruct((2, EARLY * FRAMES, HD), F32)
    q = jax.ShapeDtypeStruct((2, EARLY, HD, FRAMES), F32)
    return pl.pallas_call(
        early_kernel,
        out_shape=(kv, kv, q),
        in_specs=[ANY] * (2 * EARLY),
        out_specs=(VMEM,) * 3,
        scratch_shapes=chunk_scratch(EARLY),
        compiler_params=pltpu.CompilerParams(vmem_limit_bytes=40 * MIB),
        cost_estimate=pl.CostEstimate(flops=5_000_000_000, bytes_accessed=8_000_000, transcendentals=2_000_000),
    )(*xs, *ys)


def late_tiles(xs, ys, partial, gw):
    shapes = [jax.ShapeDtypeStruct((FRAMES + GW_OUT, 3 * HD), F32 if s == 0 else BF16) for s in range(SIDE)] * 2
    acc = pltpu.VMEM((2, SIDE * FRAMES, HD), F32)
    out = pl.pallas_call(
        late_kernel,
        out_shape=tuple(shapes),
        in_specs=[ANY] * 8 + [VMEM] * 5,
        out_specs=(VMEM,) * 8,
        scratch_shapes=[
            acc,
            acc,
            pltpu.VMEM((2, SIDE - 1, GW, 4 * HD), BF16),
            pltpu.VMEM((2, GW, 4 * HD), F32),
            pltpu.SemaphoreType.DMA((2, SIDE - 1)),
        ]
        + chunk_scratch(SIDE),
        compiler_params=pltpu.CompilerParams(vmem_limit_bytes=40 * MIB),
        cost_estimate=pl.CostEstimate(flops=5_000_000_000, bytes_accessed=8_000_000, transcendentals=2_000_000),
    )(*xs, *ys, *partial, *gw)
    return out[0:4], out[4:8]


def merge_kernel(*refs):
    xs, ys = refs[0:4], refs[4:8]
    q_ref, k_ref, v_ref, w_ref = refs[8:12]
    for out, column, first in ((q_ref, 0, 0), (k_ref, 1, 1), (v_ref, 2, 1)):
        for head in range(2):
            parts = xs if head == first else ys
            cut = slice(column * HD, (column + 1) * HD)
            total = parts[0][:FRAMES, cut]
            for part in parts[1:]:
                total = total + part[:FRAMES, cut].astype(F32)
            out[:, head * HD:(head + 1) * HD] = total.astype(BF16)
    for head, parts in ((0, xs), (1, ys)):
        total = parts[0][FRAMES:, 0:2 * HD]
        for part in parts[1:]:
            total = total + part[FRAMES:, 0:2 * HD].astype(F32)
        w_ref[0:GW_OUT, head * HD:(head + 1) * HD] = total[:, 0:HD]
        w_ref[GW_OUT:, head * HD:(head + 1) * HD] = total[:, HD:]


def merge(xs, ys):
    shape = jax.ShapeDtypeStruct((FRAMES, 2 * HD), BF16)
    return pl.pallas_call(
        merge_kernel,
        out_shape=(shape, shape, shape, jax.ShapeDtypeStruct((GW, 2 * HD), F32)),
        compiler_params=pltpu.CompilerParams(vmem_limit_bytes=32 * MIB),
        cost_estimate=pl.CostEstimate(flops=2_000_000, bytes_accessed=4_000_000, transcendentals=0),
    )(*xs, *ys)


def shards(queries, keys, values, attn_out, lse, out_grad, w_out, block_utt):
    own_x, own_y, px, py = pack(queries, keys, values, attn_out, lse, out_grad, w_out, block_utt)
    near = [along_x(px[0], 1), along_y(py[0], 1), along_x(px[1], 3), along_y(py[1], 3)]
    held = hold(px[2], py[2])
    far, held, near = lax.optimization_barrier(((px[2], py[2]), held, near))
    xs = [held[0], near[0], near[2], along_x(far[0], 2)]
    ys = [held[1], near[1], near[3], along_y(far[1], 2)]
    partial = early_tiles(xs[:EARLY], ys[:EARLY])
    ox, oy = late_tiles(xs, ys, partial, (own_x, own_y))
    bx = [ox[0]] + [along_x(ox[s], SIDE - OFFSETS[s]) for s in (1, 2, 3)]
    by = [oy[0]] + [along_y(oy[s], SIDE - OFFSETS[s]) for s in (1, 2, 3)]
    return merge(bx, by)


def solution(mesh):
    return jax.shard_map(
        shards,
        mesh=mesh,
        in_specs=(
            P(("dp", "ctx"), "head"),
            P(("dp", "ctx"), "head"),
            P(("dp", "ctx"), "head"),
            P(("dp", "ctx"), "head"),
            P("head", ("dp", "ctx")),
            P(("dp", "ctx"), None),
            P("head", None),
            P(("dp", "ctx")),
        ),
        out_specs=(
            P(("dp", "ctx"), "head"),
            P(("dp", "ctx"), "head"),
            P(("dp", "ctx"), "head"),
            P("ctx", ("dp", "head")),
        ),
        check_vma=False,
    )
```

```python
import functools
import math

import jax
import jax.numpy as jnp
from jax import lax
from jax.experimental import pallas as pl
from jax.experimental.pallas import tpu as pltpu
from jax.sharding import PartitionSpec as P

SIDE = 4
OFFSETS = (0, 1, 3, 2)
EARLY = 3
HD = 128
BLOCK = 128
FRAMES = 512
BLOCKS = FRAMES // BLOCK
WIDTH = 1024
EXTRA = 16
GROUP = 4
LOG2E = math.log2(math.e)
SCALE = 1.0 / math.sqrt(HD)
F32 = jnp.float32
BF16 = jnp.bfloat16
NT = (((1,), (1,)), ((), ()))
NN = (((1,), (0,)), ((), ()))
TN = (((0,), (0,)), ((), ()))
ANY = pl.BlockSpec(memory_space=pl.ANY)
VMEM = pl.BlockSpec(memory_space=pltpu.VMEM)
SMEM = pl.BlockSpec(memory_space=pltpu.SMEM)
GW = WIDTH // SIDE // SIDE
GW_OUT = GW // 2
MIB = 1024 * 1024


def along_x(shard, by):
    pairs = [(y * SIDE + x, y * SIDE + (x + by) % SIDE) for y in range(SIDE) for x in range(SIDE)]
    return lax.ppermute(shard, "ctx", pairs)


def along_y(shard, by):
    pairs = [(y * SIDE + x, ((y + by) % SIDE) * SIDE + x) for y in range(SIDE) for x in range(SIDE)]
    return lax.ppermute(shard, "ctx", pairs)


def dot(a, b, dims):
    return lax.dot_general(a, b, dims, preferred_element_type=F32)


def in_three(row):
    high = row.astype(BF16)
    rest = row - high.astype(F32)
    middle = rest.astype(BF16)
    low = (rest - middle.astype(F32)).astype(BF16)
    return [high, middle, low]


def fetch(pairs, sem):
    copies = [pltpu.make_async_copy(a, b, sem.at[i]) for i, (a, b) in enumerate(pairs)]
    for copy in copies:
        copy.start()
    return copies


def pack_kernel(ids_ref, lse_ref, og_hbm, w_hbm, o_hbm, q_hbm, k_hbm, v_hbm, *refs):
    own = refs[0:2]
    sent = (refs[2:5], refs[5:8])
    og, w, o, whole, body, low, sem, out_sem = refs[8:]
    ins = [(og_hbm, og), (w_hbm, w), (o_hbm, o)]
    rows = pl.ds(0, FRAMES)
    for head in range(2):
        mine = pl.ds(head * HD, HD)
        other = pl.ds((1 - head) * HD, HD)
        ins.append((q_hbm.at[:, mine], body.at[head, rows, pl.ds(0, HD)]))
        ins.append((k_hbm.at[:, other], body.at[head, rows, pl.ds(2 * HD, HD)]))
        ins.append((v_hbm.at[:, other], body.at[head, rows, pl.ds(3 * HD, HD)]))
    copies = fetch(ins, sem)
    lane = lax.broadcasted_iota(jnp.int32, (1, FRAMES), 1) // BLOCK
    ids = jnp.where(
        lane < 2,
        jnp.where(lane == 0, ids_ref[0], ids_ref[1]),
        jnp.where(lane == 2, ids_ref[2], ids_ref[3]),
    ).astype(F32).astype(BF16)
    copies[0].wait()
    copies[1].wait()
    grad_o = dot(og[...], w[...], NT).astype(BF16)
    copies[2].wait()
    prod = grad_o.astype(F32) * o[...].astype(F32)
    for copy in copies[3:]:
        copy.wait()
    outs = []
    top, bottom = pl.ds(0, FRAMES + EXTRA), pl.ds(FRAMES + EXTRA, GW)
    for head in range(2):
        mine = slice(head * HD, (head + 1) * HD)
        body[head, :FRAMES, HD:2 * HD] = grad_o[:, mine]
        delta = jnp.sum(prod[:, mine].T, axis=0, keepdims=True)
        lse = lse_ref[head:head + 1, :] * F32(LOG2E)
        extra = in_three(lse) + in_three(delta) + [ids]
        extra.append(jnp.zeros((EXTRA - len(extra), FRAMES), BF16))
        body[head, FRAMES:, :] = jnp.concatenate(extra, axis=0)
        outs += fetch([(body.at[head], out.at[top]) for out in sent[head]], out_sem.at[head])
    whole[...] = dot(og[...], o[...], TN)
    me = (lax.rem(lax.axis_index("ctx"), SIDE), lax.axis_index("ctx") // SIDE)
    for i in range(2):
        for n, r in enumerate((0,) + OFFSETS[1:]):
            to = lax.rem(me[i] + r, SIDE)
            for part in range(SIDE):
                at = (part * SIDE + to if i == 0 else to * SIDE + part) * GW
                piece = whole[pl.ds(pl.multiple_of(at, GW), GW), (1 - i) * HD:(2 - i) * HD]
                cut = slice(part * HD, (part + 1) * HD)
                if n == 0:
                    own[i][:, cut] = piece
                else:
                    low[i, n - 1, :, cut] = piece.astype(BF16)
        outs += fetch([(low.at[i, n], out.at[bottom]) for n, out in enumerate(sent[i])], out_sem.at[2 + i])
    for copy in outs:
        copy.wait()


def pack(q, k, v, o, lse, og, w, ids):
    sent = jax.ShapeDtypeStruct((FRAMES + EXTRA + GW, 4 * HD), BF16)
    own = jax.ShapeDtypeStruct((GW, 4 * HD), F32)
    out = pl.pallas_call(
        pack_kernel,
        out_shape=(own, own) + (sent,) * 6,
        in_specs=[SMEM, VMEM] + [ANY] * 6,
        out_specs=(VMEM, VMEM) + (ANY,) * 6,
        scratch_shapes=[
            pltpu.VMEM((FRAMES, WIDTH), BF16),
            pltpu.VMEM((2 * HD, WIDTH), BF16),
            pltpu.VMEM((FRAMES, 2 * HD), BF16),
            pltpu.VMEM((WIDTH, 2 * HD), F32),
            pltpu.VMEM((2, FRAMES + EXTRA, 4 * HD), BF16),
            pltpu.VMEM((2, SIDE - 1, GW, 4 * HD), BF16),
            pltpu.SemaphoreType.DMA((9,)),
            pltpu.SemaphoreType.DMA((4, SIDE - 1)),
        ],
        compiler_params=pltpu.CompilerParams(vmem_limit_bytes=58 * MIB),
        cost_estimate=pl.CostEstimate(flops=540_000_000, bytes_accessed=6_000_000, transcendentals=0),
    )(ids, lse, og, w, o, q, k, v)
    return out[0], out[1], out[2:5], out[5:8]


def load_chunks(slots, xs, ys, qd, ks, vs, extras, rows, ids_v, ids_s, sem, id_sem):
    copies = []
    for s in range(slots):
        span = pl.ds(s * FRAMES, FRAMES)
        top = pl.ds(0, FRAMES)
        bottom = pl.ds(FRAMES, EXTRA)
        for head, qsrc, ksrc in ((0, xs[s], ys[s]), (1, ys[s], xs[s])):
            copies += fetch(
                [
                    (qsrc.at[bottom, :], extras.at[head, s]),
                    (qsrc.at[top, pl.ds(0, 2 * HD)], qd.at[head, span]),
                    (ksrc.at[top, pl.ds(2 * HD, HD)], ks.at[head, span]),
                    (ksrc.at[top, pl.ds(3 * HD, HD)], vs.at[head, span]),
                ],
                sem.at[2 * s + head],
            )
    for copy in copies[0::4]:
        copy.wait()
    for s in range(slots):
        for head in range(2):
            extra = extras[head, s].astype(F32)
            rows[head, s, 0:1, :] = extra[0:1] + extra[1:2] + extra[2:3]
            rows[head, s, 1:2, :] = extra[3:4] + extra[4:5] + extra[5:6]
            rows[head, s, 2:3, :] = extra[6:7]
            ids_v[head * SIDE + s:head * SIDE + s + 1, :] = extra[6:7].astype(jnp.int32)
    to_scalars = pltpu.make_async_copy(ids_v, ids_s, id_sem)
    to_scalars.start()
    return copies, to_scalars


def run_chunk(head, s, k_slots, dq_t, qd, ks, vs, rows, ids_s, live, dk, dv):
    q_row, k_row = head * SIDE, (1 - head) * SIDE
    q_ids = [ids_s[q_row + s, j * BLOCK] for j in range(BLOCKS)]
    n = jnp.int32(0)
    for ks_slot in k_slots:
        for j in range(BLOCKS):
            kid = ids_s[k_row + ks_slot, j * BLOCK]
            hit = (kid == q_ids[0]) | (kid == q_ids[1]) | (kid == q_ids[2]) | (kid == q_ids[3])
            live[0, n] = ks_slot * BLOCKS + j
            live[1, n] = kid
            n = n + hit.astype(jnp.int32)
    for pad in range(GROUP - 1):
        live[0, n + pad] = k_slots[0] * BLOCKS
        live[1, n + pad] = -1
    span = pl.ds(s * FRAMES, FRAMES)
    lse = rows[head, s, 0:1, :]
    delta = rows[head, s, 1:2, :]
    ids_row = rows[head, s, 2:3, :].astype(jnp.int32)

    def unit(size, parts, first, g, total):
        query = qd[head, span, 0:HD]
        grad = qd[head, span, HD:2 * HD]
        spans = []
        kids = []
        for j in range(size):
            at = live[0, first + g * size + j]
            spans.append(pl.ds(pl.multiple_of(at * BLOCK, BLOCK), BLOCK))
            kids.append(live[1, first + g * size + j])
        key = jnp.concatenate([ks[head, p, :] for p in spans], axis=0)
        value = jnp.concatenate([vs[head, p, :] for p in spans], axis=0)
        wide = FRAMES // parts
        cuts = [slice(c * wide, (c + 1) * wide) for c in range(parts)]
        fronts = [(dot(key, query[c], NT), dot(value, grad[c], NT)) for c in cuts]
        add_v = add_k = None
        add_q = []
        for c, (scores, dprob) in zip(cuts, fronts):
            probs = []
            dscores = []
            for j in range(size):
                cut = slice(j * BLOCK, (j + 1) * BLOCK)
                prob = jnp.exp2(scores[cut] * F32(SCALE * LOG2E) - lse[:, c])
                prob = jnp.where(ids_row[:, c] == kids[j], prob, F32(0.0))
                probs.append(prob.astype(BF16))
                dscores.append((prob * (dprob[cut] - delta[:, c])).astype(BF16))
            prob_b = jnp.concatenate(probs, axis=0)
            dscore = jnp.concatenate(dscores, axis=0)
            part_v = dot(prob_b, grad[c], NN)
            part_k = dot(dscore, query[c], NN)
            add_v = part_v if add_v is None else add_v + part_v
            add_k = part_k if add_k is None else add_k + part_k
            add_q.append(dot(key, dscore, TN))
        for j in range(size):
            cut = slice(j * BLOCK, (j + 1) * BLOCK)
            dv[head, spans[j], :] += add_v[cut]
            dk[head, spans[j], :] += add_k[cut]
        return total + jnp.concatenate(add_q, axis=1)

    rest = lax.rem(n, GROUP)
    groups = n // GROUP + (rest == GROUP - 1).astype(jnp.int32)
    dq_t = lax.fori_loop(0, groups, functools.partial(unit, GROUP, 2, 0), dq_t)
    small = ((rest == 1) | (rest == 2)).astype(jnp.int32)
    return lax.fori_loop(0, small, functools.partial(unit, GROUP // 2, 1, groups * GROUP), dq_t)


def own_kernel(px, py, hx, hy, dk, dv, dq_t, *scratch):
    qd, ks, vs, extras, rows, ids_v, ids_s, live, sem, id_sem, hold_sem = scratch
    top = pl.ds(0, FRAMES + EXTRA)
    holds = fetch([(px.at[top], hx), (py.at[top], hy)], hold_sem)
    copies, to_scalars = load_chunks(1, (px,), (py,), qd, ks, vs, extras, rows, ids_v, ids_s, sem, id_sem)
    dk[...] = jnp.zeros_like(dk)
    dv[...] = jnp.zeros_like(dv)
    to_scalars.wait()
    for i, copy in enumerate(copies):
        if i % 4:
            copy.wait()
    for head in range(2):
        zero = jnp.zeros((HD, FRAMES), F32)
        dq_t[head, 0] = run_chunk(head, 0, (0,), zero, qd, ks, vs, rows, ids_s, live, dk, dv)
    for copy in holds:
        copy.wait()


def early_kernel(*refs):
    xs, ys = refs[0:EARLY], refs[EARLY:2 * EARLY]
    old_k, old_v, old_q = refs[2 * EARLY:2 * EARLY + 3]
    dk, dv, dq_t = refs[2 * EARLY + 3:2 * EARLY + 6]
    qd, ks, vs, extras, rows, ids_v, ids_s, live, sem, id_sem = refs[2 * EARLY + 6:]
    copies, to_scalars = load_chunks(EARLY, xs, ys, qd, ks, vs, extras, rows, ids_v, ids_s, sem, id_sem)
    dk[:, 0:FRAMES, :] = old_k[...]
    dv[:, 0:FRAMES, :] = old_v[...]
    dk[:, FRAMES:, :] = jnp.zeros_like(dk[:, FRAMES:, :])
    dv[:, FRAMES:, :] = jnp.zeros_like(dv[:, FRAMES:, :])
    to_scalars.wait()
    for i, copy in enumerate(copies):
        if i % 4:
            copy.wait()
    for s in range(EARLY):
        for head in range(2):
            start = old_q[head, 0] if s == 0 else jnp.zeros((HD, FRAMES), F32)
            k_slots = range(1, EARLY) if s == 0 else range(EARLY)
            dq_t[head, s] = run_chunk(head, s, k_slots, start, qd, ks, vs, rows, ids_s, live, dk, dv)


def late_kernel(*refs):
    xs, ys = refs[0:4], refs[4:8]
    old_k, old_v, old_q = refs[8:11]
    gw_own = refs[11:13]
    ox, oy = refs[13:17], refs[17:21]
    dk, dv, gw_in, gw_sum, gw_sem, qd, ks, vs, extras, rows, ids_v, ids_s, live, sem, id_sem = refs[21:]
    low = pl.ds(FRAMES + EXTRA, GW)
    gw_copies = []
    for i, parts in enumerate((xs, ys)):
        gw_copies += fetch([(part.at[low], gw_in.at[i, n]) for n, part in enumerate(parts[1:])], gw_sem.at[i])
    copies, to_scalars = load_chunks(SIDE, xs, ys, qd, ks, vs, extras, rows, ids_v, ids_s, sem, id_sem)
    done = EARLY * FRAMES
    dk[:, 0:done, :] = old_k[...]
    dv[:, 0:done, :] = old_v[...]
    dk[:, done:, :] = jnp.zeros_like(dk[:, done:, :])
    dv[:, done:, :] = jnp.zeros_like(dv[:, done:, :])
    me = (lax.rem(lax.axis_index("ctx"), SIDE), lax.axis_index("ctx") // SIDE)
    for copy in gw_copies:
        copy.wait()
    for i in range(2):
        total = gw_own[i][...]
        for n in range(SIDE - 1):
            total = total + gw_in[i, n].astype(F32)
        gw_sum[i] = total
    for s in range(SIDE):
        for i, out in ((1, ox[s]), (0, oy[s])):
            at = lax.rem(me[1 - i] + SIDE - OFFSETS[s], SIDE) * HD
            cut = pl.ds(pl.multiple_of(at, HD), HD)
            out[FRAMES:, 0:HD] = gw_sum[i, 0:GW_OUT, cut].astype(out.dtype)
            out[FRAMES:, HD:2 * HD] = gw_sum[i, GW_OUT:GW, cut].astype(out.dtype)
            out[FRAMES:, 2 * HD:] = jnp.zeros((GW_OUT, HD), out.dtype)
    to_scalars.wait()
    for i, copy in enumerate(copies):
        if i % 4:
            copy.wait()
    for s in range(SIDE):
        for head, out in ((0, ox[s]), (1, oy[s])):
            early = s < EARLY
            start = old_q[head, s] if early else jnp.zeros((HD, FRAMES), F32)
            k_slots = range(EARLY, SIDE) if early else range(SIDE)
            dq_t = run_chunk(head, s, k_slots, start, qd, ks, vs, rows, ids_s, live, dk, dv)
            out[:FRAMES, 0:HD] = (dq_t.T * F32(SCALE)).astype(out.dtype)
    for s in range(SIDE):
        span = pl.ds(s * FRAMES, FRAMES)
        for head, out in ((1, ox[s]), (0, oy[s])):
            out[:FRAMES, HD:2 * HD] = (dk[head, span, :] * F32(SCALE)).astype(out.dtype)
            out[:FRAMES, 2 * HD:3 * HD] = dv[head, span, :].astype(out.dtype)


def chunk_scratch(slots):
    whole = slots * FRAMES
    return [
        pltpu.VMEM((2, whole, 2 * HD), BF16),
        pltpu.VMEM((2, whole, HD), BF16),
        pltpu.VMEM((2, whole, HD), BF16),
        pltpu.VMEM((2, slots, EXTRA, FRAMES), BF16),
        pltpu.VMEM((2, slots, 8, FRAMES), F32),
        pltpu.VMEM((2 * SIDE, FRAMES), jnp.int32),
        pltpu.SMEM((2 * SIDE, FRAMES), jnp.int32),
        pltpu.SMEM((2, SIDE * BLOCKS + GROUP), jnp.int32),
        pltpu.SemaphoreType.DMA((2 * slots, 4)),
        pltpu.SemaphoreType.DMA,
    ]


def own_tiles(px, py):
    held = jax.ShapeDtypeStruct((FRAMES + EXTRA, 4 * HD), BF16)
    kv = jax.ShapeDtypeStruct((2, FRAMES, HD), F32)
    q = jax.ShapeDtypeStruct((2, 1, HD, FRAMES), F32)
    out = pl.pallas_call(
        own_kernel,
        out_shape=(held, held, kv, kv, q),
        in_specs=[ANY] * 2,
        out_specs=(VMEM,) * 5,
        scratch_shapes=chunk_scratch(1) + [pltpu.SemaphoreType.DMA((2,))],
        compiler_params=pltpu.CompilerParams(vmem_limit_bytes=40 * MIB),
        cost_estimate=pl.CostEstimate(flops=700_000_000, bytes_accessed=4_000_000, transcendentals=500_000),
    )(px, py)
    return out[0:2], out[2:5]


def early_tiles(xs, ys, partial):
    kv = jax.ShapeDtypeStruct((2, EARLY * FRAMES, HD), F32)
    q = jax.ShapeDtypeStruct((2, EARLY, HD, FRAMES), F32)
    return pl.pallas_call(
        early_kernel,
        out_shape=(kv, kv, q),
        in_specs=[ANY] * (2 * EARLY) + [VMEM] * 3,
        out_specs=(VMEM,) * 3,
        scratch_shapes=chunk_scratch(EARLY),
        compiler_params=pltpu.CompilerParams(vmem_limit_bytes=40 * MIB),
        cost_estimate=pl.CostEstimate(flops=5_000_000_000, bytes_accessed=8_000_000, transcendentals=2_000_000),
    )(*xs, *ys, *partial)


def late_tiles(xs, ys, partial, gw):
    shapes = [jax.ShapeDtypeStruct((FRAMES + GW_OUT, 3 * HD), F32 if s == 0 else BF16) for s in range(SIDE)] * 2
    acc = pltpu.VMEM((2, SIDE * FRAMES, HD), F32)
    out = pl.pallas_call(
        late_kernel,
        out_shape=tuple(shapes),
        in_specs=[ANY] * 8 + [VMEM] * 5,
        out_specs=(VMEM,) * 8,
        scratch_shapes=[
            acc,
            acc,
            pltpu.VMEM((2, SIDE - 1, GW, 4 * HD), BF16),
            pltpu.VMEM((2, GW, 4 * HD), F32),
            pltpu.SemaphoreType.DMA((2, SIDE - 1)),
        ]
        + chunk_scratch(SIDE),
        compiler_params=pltpu.CompilerParams(vmem_limit_bytes=40 * MIB),
        cost_estimate=pl.CostEstimate(flops=5_000_000_000, bytes_accessed=8_000_000, transcendentals=2_000_000),
    )(*xs, *ys, *partial, *gw)
    return out[0:4], out[4:8]


def merge_kernel(*refs):
    xs, ys = refs[0:4], refs[4:8]
    q_ref, k_ref, v_ref, w_ref = refs[8:12]
    for out, column, first in ((q_ref, 0, 0), (k_ref, 1, 1), (v_ref, 2, 1)):
        for head in range(2):
            parts = xs if head == first else ys
            cut = slice(column * HD, (column + 1) * HD)
            total = parts[0][:FRAMES, cut]
            for part in parts[1:]:
                total = total + part[:FRAMES, cut].astype(F32)
            out[:, head * HD:(head + 1) * HD] = total.astype(BF16)
    for head, parts in ((0, xs), (1, ys)):
        total = parts[0][FRAMES:, 0:2 * HD]
        for part in parts[1:]:
            total = total + part[FRAMES:, 0:2 * HD].astype(F32)
        w_ref[0:GW_OUT, head * HD:(head + 1) * HD] = total[:, 0:HD]
        w_ref[GW_OUT:, head * HD:(head + 1) * HD] = total[:, HD:]


def merge(xs, ys):
    shape = jax.ShapeDtypeStruct((FRAMES, 2 * HD), BF16)
    return pl.pallas_call(
        merge_kernel,
        out_shape=(shape, shape, shape, jax.ShapeDtypeStruct((GW, 2 * HD), F32)),
        compiler_params=pltpu.CompilerParams(vmem_limit_bytes=32 * MIB),
        cost_estimate=pl.CostEstimate(flops=2_000_000, bytes_accessed=4_000_000, transcendentals=0),
    )(*xs, *ys)


def shards(queries, keys, values, attn_out, lse, out_grad, w_out, block_utt):
    own_x, own_y, px, py = pack(queries, keys, values, attn_out, lse, out_grad, w_out, block_utt)
    near = [along_x(px[0], 1), along_y(py[0], 1), along_x(px[1], 3), along_y(py[1], 3)]
    held, partial = own_tiles(px[2], py[2])
    far_x, far_y, held, partial = lax.optimization_barrier((px[2], py[2], held, partial))
    xs = [held[0], near[0], near[2], along_x(far_x, 2)]
    ys = [held[1], near[1], near[3], along_y(far_y, 2)]
    partial = early_tiles(xs[:EARLY], ys[:EARLY], partial)
    ox, oy = late_tiles(xs, ys, partial, (own_x, own_y))
    bx, by = [ox[0]], [oy[0]]
    for s in (3, 1, 2):
        bx.append(along_x(ox[s], SIDE - OFFSETS[s]))
        by.append(along_y(oy[s], SIDE - OFFSETS[s]))
    return merge(bx, by)


def solution(mesh):
    return jax.shard_map(
        shards,
        mesh=mesh,
        in_specs=(
            P(("dp", "ctx"), "head"),
            P(("dp", "ctx"), "head"),
            P(("dp", "ctx"), "head"),
            P(("dp", "ctx"), "head"),
            P("head", ("dp", "ctx")),
            P(("dp", "ctx"), None),
            P("head", None),
            P(("dp", "ctx")),
        ),
        out_specs=(
            P(("dp", "ctx"), "head"),
            P(("dp", "ctx"), "head"),
            P(("dp", "ctx"), "head"),
            P("ctx", ("dp", "head")),
        ),
        check_vma=False,
    )
```

```python
import functools
import math

import jax
import jax.numpy as jnp
from jax import lax
from jax.experimental import pallas as pl
from jax.experimental.pallas import tpu as pltpu
from jax.sharding import PartitionSpec as P

SIDE = 4
OFFSETS = (0, 1, 3, 2)
EARLY = 3
HD = 128
BLOCK = 128
FRAMES = 512
BLOCKS = FRAMES // BLOCK
WIDTH = 1024
EXTRA = 16
LISTED = 160
GROUP = 4
LOG2E = math.log2(math.e)
SCALE = 1.0 / math.sqrt(HD)
F32 = jnp.float32
BF16 = jnp.bfloat16
NT = (((1,), (1,)), ((), ()))
NN = (((1,), (0,)), ((), ()))
TN = (((0,), (0,)), ((), ()))
ANY = pl.BlockSpec(memory_space=pl.ANY)
VMEM = pl.BlockSpec(memory_space=pltpu.VMEM)
SMEM = pl.BlockSpec(memory_space=pltpu.SMEM)
GW = WIDTH // SIDE // SIDE
GW_IN = 2 * GW
MIB = 1024 * 1024


def along_x(shard, by):
    pairs = [(y * SIDE + x, y * SIDE + (x + by) % SIDE) for y in range(SIDE) for x in range(SIDE)]
    return lax.ppermute(shard, "ctx", pairs)


def along_y(shard, by):
    pairs = [(y * SIDE + x, ((y + by) % SIDE) * SIDE + x) for y in range(SIDE) for x in range(SIDE)]
    return lax.ppermute(shard, "ctx", pairs)


def dot(a, b, dims):
    return lax.dot_general(a, b, dims, preferred_element_type=F32)


def in_three(row):
    high = row.astype(BF16)
    rest = row - high.astype(F32)
    middle = rest.astype(BF16)
    low = (rest - middle.astype(F32)).astype(BF16)
    return [high, middle, low]


def fetch(pairs, sem):
    copies = [pltpu.make_async_copy(a, b, sem.at[i]) for i, (a, b) in enumerate(pairs)]
    for copy in copies:
        copy.start()
    return copies


def finish(copies):
    for copy in copies:
        copy.wait()


def pack_kernel(ids_ref, lse_ref, og_hbm, w_hbm, o_hbm, q_hbm, k_hbm, v_hbm, *refs):
    own = refs[0]
    sent = (refs[1:4], refs[4:7])
    og, w, o, whole, body, low, sem, out_sem = refs[7:]
    ins = [(og_hbm, og), (w_hbm, w), (o_hbm, o)]
    rows = pl.ds(0, FRAMES)
    for head in range(2):
        mine = pl.ds(head * HD, HD)
        other = pl.ds((1 - head) * HD, HD)
        ins.append((q_hbm.at[:, mine], body.at[head, rows, pl.ds(0, HD)]))
        ins.append((k_hbm.at[:, other], body.at[head, rows, pl.ds(2 * HD, HD)]))
        ins.append((v_hbm.at[:, other], body.at[head, rows, pl.ds(3 * HD, HD)]))
    copies = fetch(ins, sem)
    lane = lax.broadcasted_iota(jnp.int32, (1, FRAMES), 1) // BLOCK
    ids = jnp.where(
        lane < 2,
        jnp.where(lane == 0, ids_ref[0], ids_ref[1]),
        jnp.where(lane == 2, ids_ref[2], ids_ref[3]),
    ).astype(F32).astype(BF16)
    copies[0].wait()
    copies[1].wait()
    grad_o = dot(og[...], w[...], NT).astype(BF16)
    copies[2].wait()
    prod = grad_o.astype(F32) * o[...].astype(F32)
    for copy in copies[3:]:
        copy.wait()
    outs = []
    top, bottom = pl.ds(0, FRAMES + EXTRA), pl.ds(FRAMES + EXTRA, GW_IN)
    for head in range(2):
        mine = slice(head * HD, (head + 1) * HD)
        body[head, :FRAMES, HD:2 * HD] = grad_o[:, mine]
        delta = jnp.sum(prod[:, mine].T, axis=0, keepdims=True)
        lse = lse_ref[head:head + 1, :] * F32(LOG2E)
        extra = in_three(lse) + in_three(delta) + [ids]
        extra.append(jnp.zeros((EXTRA - len(extra), FRAMES), BF16))
        body[head, FRAMES:, :] = jnp.concatenate(extra, axis=0)
        outs += fetch([(body.at[head], out.at[top]) for out in sent[head]], out_sem.at[head])
    whole[...] = dot(og[...], o[...], TN)
    y = lax.axis_index("ctx") // SIDE
    for n, r in enumerate(OFFSETS):
        to = lax.rem(y + r, SIDE)
        for part in range(SIDE):
            at = pl.multiple_of((to * SIDE + part) * GW, GW)
            cut = slice(part * HD, (part + 1) * HD)
            for half in range(2):
                piece = whole[pl.ds(at, GW), half * HD:(half + 1) * HD]
                rows = slice(half * GW, (half + 1) * GW)
                if n == 0:
                    own[rows, cut] = piece
                else:
                    low[n - 1, rows, cut] = piece.astype(BF16)
        if n:
            outs += fetch([(low.at[n - 1], sent[1][n - 1].at[bottom])], out_sem.at[2, pl.ds(n - 1, 1)])
    for copy in outs:
        copy.wait()


def pack(q, k, v, o, lse, og, w, ids):
    sent_y = jax.ShapeDtypeStruct((FRAMES + EXTRA + GW_IN, 4 * HD), BF16)
    sent_x = jax.ShapeDtypeStruct((FRAMES + EXTRA, 4 * HD), BF16)
    own = jax.ShapeDtypeStruct((GW_IN, 4 * HD), F32)
    out = pl.pallas_call(
        pack_kernel,
        out_shape=(own,) + (sent_x,) * 3 + (sent_y,) * 3,
        in_specs=[SMEM, VMEM] + [ANY] * 6,
        out_specs=(VMEM,) + (ANY,) * 6,
        scratch_shapes=[
            pltpu.VMEM((FRAMES, WIDTH), BF16),
            pltpu.VMEM((2 * HD, WIDTH), BF16),
            pltpu.VMEM((FRAMES, 2 * HD), BF16),
            pltpu.VMEM((WIDTH, 2 * HD), F32),
            pltpu.VMEM((2, FRAMES + EXTRA, 4 * HD), BF16),
            pltpu.VMEM((SIDE - 1, GW_IN, 4 * HD), BF16),
            pltpu.SemaphoreType.DMA((9,)),
            pltpu.SemaphoreType.DMA((3, SIDE - 1)),
        ],
        compiler_params=pltpu.CompilerParams(vmem_limit_bytes=58 * MIB),
        cost_estimate=pl.CostEstimate(flops=540_000_000, bytes_accessed=6_000_000, transcendentals=0),
    )(ids, lse, og, w, o, q, k, v)
    return out[0], out[1:4], out[4:7]


def load_chunks(slots, xs, ys, qd, ks, vs, extras, rows, ids_v, ids_s, sem, id_sem):
    copies = []
    for s in range(slots):
        top = pl.ds(0, FRAMES)
        bottom = pl.ds(FRAMES, EXTRA)
        for head, qsrc, ksrc in ((0, xs[s], ys[s]), (1, ys[s], xs[s])):
            flat = head * slots + s
            span = pl.ds(flat * FRAMES, FRAMES)
            copies += fetch(
                [
                    (qsrc.at[bottom, :], extras.at[flat]),
                    (qsrc.at[top, pl.ds(0, 2 * HD)], qd.at[flat]),
                    (ksrc.at[top, pl.ds(2 * HD, HD)], ks.at[span]),
                    (ksrc.at[top, pl.ds(3 * HD, HD)], vs.at[span]),
                ],
                sem.at[2 * s + head],
            )
    for copy in copies[0::4]:
        copy.wait()
    for s in range(slots):
        for head in range(2):
            flat = head * slots + s
            extra = extras[flat].astype(F32)
            rows[flat, 0:1, :] = extra[0:1] + extra[1:2] + extra[2:3]
            rows[flat, 1:2, :] = extra[3:4] + extra[4:5] + extra[5:6]
            rows[flat, 2:3, :] = extra[6:7]
            ids_v[head * SIDE + s:head * SIDE + s + 1, :] = extra[6:7].astype(jnp.int32)
    to_scalars = pltpu.make_async_copy(ids_v, ids_s, id_sem)
    to_scalars.start()
    return copies, to_scalars


def run_pairs(pairs, slots, qd, ks, vs, rows, ids_s, live, dk, dv, dq_t):
    many = jnp.int32(0)
    pair = jnp.int32(0)
    for head, s, k_slots in pairs:
        flat = head * slots + s
        q_row, k_row = head * SIDE, (1 - head) * SIDE
        q_ids = [ids_s[q_row + s, j * BLOCK] for j in range(BLOCKS)]
        n = jnp.int32(0)
        for k_slot in k_slots:
            for j in range(BLOCKS):
                kid = ids_s[k_row + k_slot, j * BLOCK]
                hit = (kid == q_ids[0]) | (kid == q_ids[1]) | (kid == q_ids[2]) | (kid == q_ids[3])
                live[0, many * GROUP + n] = (head * slots + k_slot) * BLOCKS + j
                live[1, many * GROUP + n] = kid
                n = n + hit.astype(jnp.int32)
        for pad in range(GROUP - 1):
            live[0, many * GROUP + n + pad] = head * slots * BLOCKS
            live[1, many * GROUP + n + pad] = -1
        rest = lax.rem(n, GROUP)
        groups = n // GROUP + (rest == GROUP - 1).astype(jnp.int32)
        small = ((rest == 1) | (rest == 2)).astype(jnp.int32)
        for g in range(SIDE):
            live[4, many + g] = flat
        live[5, pair] = flat
        many = many + groups
        for j in range(GROUP // 2):
            live[2, pair * (GROUP // 2) + j] = live[0, many * GROUP + j]
            live[3, pair * (GROUP // 2) + j] = live[1, many * GROUP + j]
        pair = pair + small

    def unit(size, parts, row, g, carry):
        flat = live[4 + row // 2, g]
        query = qd[flat, :, 0:HD]
        grad = qd[flat, :, HD:2 * HD]
        lse = rows[flat, 0:1, :]
        delta = rows[flat, 1:2, :]
        ids_row = rows[flat, 2:3, :].astype(jnp.int32)
        spans = []
        kids = []
        for j in range(size):
            at = live[row, g * size + j]
            spans.append(pl.ds(pl.multiple_of(at * BLOCK, BLOCK), BLOCK))
            kids.append(live[row + 1, g * size + j])
        key = jnp.concatenate([ks[p, :] for p in spans], axis=0)
        value = jnp.concatenate([vs[p, :] for p in spans], axis=0)
        wide = FRAMES // parts
        cuts = [slice(c * wide, (c + 1) * wide) for c in range(parts)]
        fronts = [(dot(key, query[c], NT), dot(value, grad[c], NT)) for c in cuts]
        add_v = add_k = None
        for c, (scores, dprob) in zip(cuts, fronts):
            probs = []
            dscores = []
            for j in range(size):
                cut = slice(j * BLOCK, (j + 1) * BLOCK)
                prob = jnp.exp2(scores[cut] * F32(SCALE * LOG2E) - lse[:, c])
                prob = jnp.where(ids_row[:, c] == kids[j], prob, F32(0.0))
                probs.append(prob.astype(BF16))
                dscores.append((prob * (dprob[cut] - delta[:, c])).astype(BF16))
            prob_b = jnp.concatenate(probs, axis=0)
            dscore = jnp.concatenate(dscores, axis=0)
            part_v = dot(prob_b, grad[c], NN)
            part_k = dot(dscore, query[c], NN)
            add_v = part_v if add_v is None else add_v + part_v
            add_k = part_k if add_k is None else add_k + part_k
            dq_t[flat, :, c] += dot(key, dscore, TN)
        for j in range(size):
            cut = slice(j * BLOCK, (j + 1) * BLOCK)
            dv[spans[j], :] += add_v[cut]
            dk[spans[j], :] += add_k[cut]
        return carry

    lax.fori_loop(0, many, functools.partial(unit, GROUP, 2, 0), 0)
    lax.fori_loop(0, pair, functools.partial(unit, GROUP // 2, 1, 2), 0)


def resume(before, slots, old_k, old_v, old_q, dk, dv, dq_t):
    done = before * FRAMES
    for head in range(2):
        first, last = head * slots * FRAMES, (head + 1) * slots * FRAMES
        for new, old in ((dk, old_k), (dv, old_v)):
            new[first:first + done, :] = old[head * done:(head + 1) * done, :]
            new[first + done:last, :] = jnp.zeros((last - first - done, HD), F32)
        dq_t[head * slots:head * slots + before] = old_q[head * before:(head + 1) * before]
        dq_t[head * slots + before:(head + 1) * slots] = jnp.zeros((slots - before, HD, FRAMES), F32)


def own_kernel(px, py, hx, hy, dk, dv, dq_t, *scratch):
    qd, ks, vs, extras, rows, ids_v, ids_s, live, sem, id_sem, hold_sem = scratch
    top = pl.ds(0, FRAMES + EXTRA)
    holds = fetch([(px.at[top], hx), (py.at[top], hy)], hold_sem)
    copies, to_scalars = load_chunks(1, (px,), (py,), qd, ks, vs, extras, rows, ids_v, ids_s, sem, id_sem)
    dk[...] = jnp.zeros_like(dk)
    dv[...] = jnp.zeros_like(dv)
    dq_t[...] = jnp.zeros_like(dq_t)
    to_scalars.wait()
    for i, copy in enumerate(copies):
        if i % 4:
            copy.wait()
    pairs = [(head, 0, (0,)) for head in range(2)]
    run_pairs(pairs, 1, qd, ks, vs, rows, ids_s, live, dk, dv, dq_t)
    for copy in holds:
        copy.wait()


def early_kernel(*refs):
    xs, ys = refs[0:EARLY], refs[EARLY:2 * EARLY]
    old_k, old_v, old_q = refs[2 * EARLY:2 * EARLY + 3]
    dk, dv, dq_t = refs[2 * EARLY + 3:2 * EARLY + 6]
    qd, ks, vs, extras, rows, ids_v, ids_s, live, sem, id_sem = refs[2 * EARLY + 6:]
    copies, to_scalars = load_chunks(EARLY, xs, ys, qd, ks, vs, extras, rows, ids_v, ids_s, sem, id_sem)
    resume(1, EARLY, old_k, old_v, old_q, dk, dv, dq_t)
    to_scalars.wait()
    for i, copy in enumerate(copies):
        if i % 4:
            copy.wait()
    pairs = [(head, s, range(1, EARLY) if s == 0 else range(EARLY)) for s in range(EARLY) for head in range(2)]
    run_pairs(pairs, EARLY, qd, ks, vs, rows, ids_s, live, dk, dv, dq_t)


def late_kernel(*refs):
    xs, ys = refs[0:4], refs[4:8]
    old_k, old_v, old_q = refs[8:11]
    gw_own = refs[11]
    ox, oy = refs[12:16], refs[16:20]
    dk, dv, dq_t, gw_in, gw_sum, gw_sem, qd, ks, vs, extras, rows, ids_v, ids_s, live, sem, id_sem = refs[20:]
    low = pl.ds(FRAMES + EXTRA, GW_IN)
    gw_copies = fetch([(part.at[low], gw_in.at[n]) for n, part in enumerate(ys[1:])], gw_sem)
    copies, to_scalars = load_chunks(SIDE, xs, ys, qd, ks, vs, extras, rows, ids_v, ids_s, sem, id_sem)
    resume(EARLY, SIDE, old_k, old_v, old_q, dk, dv, dq_t)
    finish(gw_copies)
    total = gw_own[...]
    for n in range(SIDE - 1):
        total = total + gw_in[n].astype(F32)
    gw_sum[...] = total
    for s in range(SIDE):
        at = lax.rem(lax.axis_index("ctx") + SIDE - OFFSETS[s], SIDE) * HD
        cut = pl.ds(pl.multiple_of(at, HD), HD)
        ox[s][FRAMES:, 0:HD] = gw_sum[0:GW, cut].astype(ox[s].dtype)
        ox[s][FRAMES:, HD:2 * HD] = gw_sum[GW:, cut].astype(ox[s].dtype)
        ox[s][FRAMES:, 2 * HD:] = jnp.zeros((GW, HD), ox[s].dtype)
    to_scalars.wait()
    for i, copy in enumerate(copies):
        if i % 4:
            copy.wait()
    pairs = [
        (head, s, range(EARLY, SIDE) if s < EARLY else range(SIDE)) for s in range(SIDE) for head in range(2)
    ]
    run_pairs(pairs, SIDE, qd, ks, vs, rows, ids_s, live, dk, dv, dq_t)
    for s in range(SIDE):
        for head, out_q, out_k in ((0, ox[s], oy[s]), (1, oy[s], ox[s])):
            flat = head * SIDE + s
            span = pl.ds(flat * FRAMES, FRAMES)
            out_q[:FRAMES, 0:HD] = (dq_t[flat].T * F32(SCALE)).astype(out_q.dtype)
            out_k[:FRAMES, HD:2 * HD] = (dk[span, :] * F32(SCALE)).astype(out_k.dtype)
            out_k[:FRAMES, 2 * HD:3 * HD] = dv[span, :].astype(out_k.dtype)


def chunk_scratch(slots):
    return [
        pltpu.VMEM((2 * slots, FRAMES, 2 * HD), BF16),
        pltpu.VMEM((2 * slots * FRAMES, HD), BF16),
        pltpu.VMEM((2 * slots * FRAMES, HD), BF16),
        pltpu.VMEM((2 * slots, EXTRA, FRAMES), BF16),
        pltpu.VMEM((2 * slots, 8, FRAMES), F32),
        pltpu.VMEM((2 * SIDE, FRAMES), jnp.int32),
        pltpu.SMEM((2 * SIDE, FRAMES), jnp.int32),
        pltpu.SMEM((6, LISTED), jnp.int32),
        pltpu.SemaphoreType.DMA((2 * slots, 4)),
        pltpu.SemaphoreType.DMA,
    ]


def own_tiles(px, py):
    held = jax.ShapeDtypeStruct((FRAMES + EXTRA, 4 * HD), BF16)
    kv = jax.ShapeDtypeStruct((2 * FRAMES, HD), F32)
    q = jax.ShapeDtypeStruct((2, HD, FRAMES), F32)
    out = pl.pallas_call(
        own_kernel,
        out_shape=(held, held, kv, kv, q),
        in_specs=[ANY] * 2,
        out_specs=(VMEM,) * 5,
        scratch_shapes=chunk_scratch(1) + [pltpu.SemaphoreType.DMA((2,))],
        compiler_params=pltpu.CompilerParams(vmem_limit_bytes=40 * MIB),
        cost_estimate=pl.CostEstimate(flops=700_000_000, bytes_accessed=4_000_000, transcendentals=500_000),
    )(px, py)
    return out[0:2], out[2:5]


def early_tiles(xs, ys, partial):
    kv = jax.ShapeDtypeStruct((2 * EARLY * FRAMES, HD), F32)
    q = jax.ShapeDtypeStruct((2 * EARLY, HD, FRAMES), F32)
    return pl.pallas_call(
        early_kernel,
        out_shape=(kv, kv, q),
        in_specs=[ANY] * (2 * EARLY) + [VMEM] * 3,
        out_specs=(VMEM,) * 3,
        scratch_shapes=chunk_scratch(EARLY),
        compiler_params=pltpu.CompilerParams(vmem_limit_bytes=40 * MIB),
        cost_estimate=pl.CostEstimate(flops=5_000_000_000, bytes_accessed=8_000_000, transcendentals=2_000_000),
    )(*xs, *ys, *partial)


def late_tiles(xs, ys, partial, gw):
    shapes = [
        jax.ShapeDtypeStruct((rows, 3 * HD), F32 if s == 0 else BF16) for rows in (FRAMES + GW, FRAMES) for s in range(SIDE)
    ]
    acc = pltpu.VMEM((2 * SIDE * FRAMES, HD), F32)
    out = pl.pallas_call(
        late_kernel,
        out_shape=tuple(shapes),
        in_specs=[ANY] * 8 + [VMEM] * 4,
        out_specs=(VMEM,) * 8,
        scratch_shapes=[
            acc,
            acc,
            pltpu.VMEM((2 * SIDE, HD, FRAMES), F32),
            pltpu.VMEM((SIDE - 1, GW_IN, 4 * HD), BF16),
            pltpu.VMEM((GW_IN, 4 * HD), F32),
            pltpu.SemaphoreType.DMA((SIDE - 1,)),
        ]
        + chunk_scratch(SIDE),
        compiler_params=pltpu.CompilerParams(vmem_limit_bytes=40 * MIB),
        cost_estimate=pl.CostEstimate(flops=5_000_000_000, bytes_accessed=8_000_000, transcendentals=2_000_000),
    )(*xs, *ys, *partial, gw)
    return out[0:4], out[4:8]


def merge_kernel(*refs):
    xs, ys = refs[0:4], refs[4:8]
    q_ref, k_ref, v_ref, w_ref = refs[8:12]
    for out, column, first in ((q_ref, 0, 0), (k_ref, 1, 1), (v_ref, 2, 1)):
        for head in range(2):
            parts = xs if head == first else ys
            cut = slice(column * HD, (column + 1) * HD)
            total = parts[0][:FRAMES, cut]
            for part in parts[1:]:
                total = total + part[:FRAMES, cut].astype(F32)
            out[:, head * HD:(head + 1) * HD] = total.astype(BF16)
    total = xs[0][FRAMES:, 0:2 * HD]
    for part in xs[1:]:
        total = total + part[FRAMES:, 0:2 * HD].astype(F32)
    w_ref[...] = total


def merge(xs, ys):
    shape = jax.ShapeDtypeStruct((FRAMES, 2 * HD), BF16)
    return pl.pallas_call(
        merge_kernel,
        out_shape=(shape, shape, shape, jax.ShapeDtypeStruct((GW, 2 * HD), F32)),
        compiler_params=pltpu.CompilerParams(vmem_limit_bytes=32 * MIB),
        cost_estimate=pl.CostEstimate(flops=2_000_000, bytes_accessed=4_000_000, transcendentals=0),
    )(*xs, *ys)


def shards(queries, keys, values, attn_out, lse, out_grad, w_out, block_utt):
    own, px, py = pack(queries, keys, values, attn_out, lse, out_grad, w_out, block_utt)
    near = [along_x(px[0], 1), along_y(py[0], 1), along_x(px[1], 3), along_y(py[1], 3)]
    held, partial = own_tiles(px[2], py[2])
    far_x, held, near[0], near[2] = lax.optimization_barrier((px[2], held, near[0], near[2]))
    far_y, partial, near[1], near[3] = lax.optimization_barrier((py[2], partial, near[1], near[3]))
    xs = [held[0], near[0], near[2], along_x(far_x, 2)]
    ys = [held[1], near[1], near[3], along_y(far_y, 2)]
    partial = early_tiles(xs[:EARLY], ys[:EARLY], partial)
    ox, oy = late_tiles(xs, ys, partial, own)
    bx, by = [ox[0]], [oy[0]]
    for s in (3, 1, 2):
        bx.append(along_x(ox[s], SIDE - OFFSETS[s]))
        by.append(along_y(oy[s], SIDE - OFFSETS[s]))
    return merge(bx, by)


def solution(mesh):
    return jax.shard_map(
        shards,
        mesh=mesh,
        in_specs=(
            P(("dp", "ctx"), "head"),
            P(("dp", "ctx"), "head"),
            P(("dp", "ctx"), "head"),
            P(("dp", "ctx"), "head"),
            P("head", ("dp", "ctx")),
            P(("dp", "ctx"), None),
            P("head", None),
            P(("dp", "ctx")),
        ),
        out_specs=(
            P(("dp", "ctx"), "head"),
            P(("dp", "ctx"), "head"),
            P(("dp", "ctx"), "head"),
            P("ctx", ("dp", "head")),
        ),
        check_vma=False,
    )
```

```python
import functools
import math

import jax
import jax.numpy as jnp
from jax import lax
from jax.experimental import pallas as pl
from jax.experimental.pallas import tpu as pltpu
from jax.sharding import PartitionSpec as P

SIDE = 4
OFFSETS = (0, 1, 3, 2)
EARLY = 3
HD = 128
BLOCK = 128
FRAMES = 512
BLOCKS = FRAMES // BLOCK
WIDTH = 1024
EXTRA = 16
LISTED = 160
GROUP = 4
LOG2E = math.log2(math.e)
SCALE = 1.0 / math.sqrt(HD)
F32 = jnp.float32
BF16 = jnp.bfloat16
NT = (((1,), (1,)), ((), ()))
NN = (((1,), (0,)), ((), ()))
TN = (((0,), (0,)), ((), ()))
ANY = pl.BlockSpec(memory_space=pl.ANY)
VMEM = pl.BlockSpec(memory_space=pltpu.VMEM)
SMEM = pl.BlockSpec(memory_space=pltpu.SMEM)
GW = WIDTH // SIDE // SIDE
GW_IN = 2 * GW
GW_OUT = 3 * GW // 4
GW_REST = GW - GW_OUT
MIB = 1024 * 1024


def along_x(shard, by):
    pairs = [(y * SIDE + x, y * SIDE + (x + by) % SIDE) for y in range(SIDE) for x in range(SIDE)]
    return lax.ppermute(shard, "ctx", pairs)


def along_y(shard, by):
    pairs = [(y * SIDE + x, ((y + by) % SIDE) * SIDE + x) for y in range(SIDE) for x in range(SIDE)]
    return lax.ppermute(shard, "ctx", pairs)


def dot(a, b, dims):
    return lax.dot_general(a, b, dims, preferred_element_type=F32)


def in_three(row):
    high = row.astype(BF16)
    rest = row - high.astype(F32)
    middle = rest.astype(BF16)
    low = (rest - middle.astype(F32)).astype(BF16)
    return [high, middle, low]


def fetch(pairs, sem):
    copies = [pltpu.make_async_copy(a, b, sem.at[i]) for i, (a, b) in enumerate(pairs)]
    for copy in copies:
        copy.start()
    return copies


def finish(copies):
    for copy in copies:
        copy.wait()


def pack_kernel(ids_ref, lse_ref, og_hbm, w_hbm, o_hbm, q_hbm, k_hbm, v_hbm, *refs):
    own = refs[0]
    sent = (refs[1:2], refs[2:5])
    og, w, o, whole, body, low, sem, out_sem = refs[5:]
    ins = [(og_hbm, og), (w_hbm, w), (o_hbm, o)]
    rows = pl.ds(0, FRAMES)
    for head in range(2):
        mine = pl.ds(head * HD, HD)
        other = pl.ds((1 - head) * HD, HD)
        ins.append((q_hbm.at[:, mine], body.at[head, rows, pl.ds(0, HD)]))
        ins.append((k_hbm.at[:, other], body.at[head, rows, pl.ds(2 * HD, HD)]))
        ins.append((v_hbm.at[:, other], body.at[head, rows, pl.ds(3 * HD, HD)]))
    copies = fetch(ins, sem)
    lane = lax.broadcasted_iota(jnp.int32, (1, FRAMES), 1) // BLOCK
    ids = jnp.where(
        lane < 2,
        jnp.where(lane == 0, ids_ref[0], ids_ref[1]),
        jnp.where(lane == 2, ids_ref[2], ids_ref[3]),
    ).astype(F32).astype(BF16)
    copies[0].wait()
    copies[1].wait()
    grad_o = dot(og[...], w[...], NT).astype(BF16)
    copies[2].wait()
    prod = grad_o.astype(F32) * o[...].astype(F32)
    for copy in copies[3:]:
        copy.wait()
    outs = []
    top, bottom = pl.ds(0, FRAMES + EXTRA), pl.ds(FRAMES + EXTRA, GW_IN)
    for head in range(2):
        mine = slice(head * HD, (head + 1) * HD)
        body[head, :FRAMES, HD:2 * HD] = grad_o[:, mine]
        delta = jnp.sum(prod[:, mine].T, axis=0, keepdims=True)
        lse = lse_ref[head:head + 1, :] * F32(LOG2E)
        extra = in_three(lse) + in_three(delta) + [ids]
        extra.append(jnp.zeros((EXTRA - len(extra), FRAMES), BF16))
        body[head, FRAMES:, :] = jnp.concatenate(extra, axis=0)
        outs += fetch([(body.at[head], out.at[top]) for out in sent[head]], out_sem.at[head])
    whole[...] = dot(og[...], o[...], TN)
    y = lax.axis_index("ctx") // SIDE
    for n, r in enumerate(OFFSETS):
        to = lax.rem(y + r, SIDE)
        for part in range(SIDE):
            at = pl.multiple_of((to * SIDE + part) * GW, GW)
            cut = slice(part * HD, (part + 1) * HD)
            for half in range(2):
                piece = whole[pl.ds(at, GW), half * HD:(half + 1) * HD]
                rows = slice(half * GW, (half + 1) * GW)
                if n == 0:
                    own[rows, cut] = piece
                else:
                    low[n - 1, rows, cut] = piece.astype(BF16)
        if n:
            outs += fetch([(low.at[n - 1], sent[1][n - 1].at[bottom])], out_sem.at[2, pl.ds(n - 1, 1)])
    for copy in outs:
        copy.wait()


def pack(q, k, v, o, lse, og, w, ids):
    sent_y = jax.ShapeDtypeStruct((FRAMES + EXTRA + GW_IN, 4 * HD), BF16)
    sent_x = jax.ShapeDtypeStruct((FRAMES + EXTRA, 4 * HD), BF16)
    own = jax.ShapeDtypeStruct((GW_IN, 4 * HD), F32)
    out = pl.pallas_call(
        pack_kernel,
        out_shape=(own, sent_x) + (sent_y,) * 3,
        in_specs=[SMEM, VMEM] + [ANY] * 6,
        out_specs=(VMEM,) + (ANY,) * 4,
        scratch_shapes=[
            pltpu.VMEM((FRAMES, WIDTH), BF16),
            pltpu.VMEM((2 * HD, WIDTH), BF16),
            pltpu.VMEM((FRAMES, 2 * HD), BF16),
            pltpu.VMEM((WIDTH, 2 * HD), F32),
            pltpu.VMEM((2, FRAMES + EXTRA, 4 * HD), BF16),
            pltpu.VMEM((SIDE - 1, GW_IN, 4 * HD), BF16),
            pltpu.SemaphoreType.DMA((9,)),
            pltpu.SemaphoreType.DMA((3, SIDE - 1)),
        ],
        compiler_params=pltpu.CompilerParams(vmem_limit_bytes=58 * MIB),
        cost_estimate=pl.CostEstimate(flops=540_000_000, bytes_accessed=6_000_000, transcendentals=0),
    )(ids, lse, og, w, o, q, k, v)
    return out[0], out[1], out[2:5]


def load_chunks(slots, xs, ys, qd, ks, vs, extras, rows, ids_v, ids_s, sem, id_sem):
    copies = []
    for s in range(slots):
        top = pl.ds(0, FRAMES)
        bottom = pl.ds(FRAMES, EXTRA)
        for head, qsrc, ksrc in ((0, xs[s], ys[s]), (1, ys[s], xs[s])):
            flat = head * slots + s
            span = pl.ds(flat * FRAMES, FRAMES)
            copies += fetch(
                [
                    (qsrc.at[bottom, :], extras.at[flat]),
                    (qsrc.at[top, pl.ds(0, 2 * HD)], qd.at[flat]),
                    (ksrc.at[top, pl.ds(2 * HD, HD)], ks.at[span]),
                    (ksrc.at[top, pl.ds(3 * HD, HD)], vs.at[span]),
                ],
                sem.at[2 * s + head],
            )
    for copy in copies[0::4]:
        copy.wait()
    for s in range(slots):
        for head in range(2):
            flat = head * slots + s
            extra = extras[flat].astype(F32)
            rows[flat, 0:1, :] = extra[0:1] + extra[1:2] + extra[2:3]
            rows[flat, 1:2, :] = extra[3:4] + extra[4:5] + extra[5:6]
            rows[flat, 2:3, :] = extra[6:7]
            ids_v[head * SIDE + s:head * SIDE + s + 1, :] = extra[6:7].astype(jnp.int32)
    to_scalars = pltpu.make_async_copy(ids_v, ids_s, id_sem)
    to_scalars.start()
    return copies, to_scalars


def run_pairs(pairs, slots, qd, ks, vs, rows, ids_s, live, dk, dv, dq_t):
    many = jnp.int32(0)
    pair = jnp.int32(0)
    for head, s, k_slots in pairs:
        flat = head * slots + s
        q_row, k_row = head * SIDE, (1 - head) * SIDE
        q_ids = [ids_s[q_row + s, j * BLOCK] for j in range(BLOCKS)]
        n = jnp.int32(0)
        for k_slot in k_slots:
            for j in range(BLOCKS):
                kid = ids_s[k_row + k_slot, j * BLOCK]
                hit = (kid == q_ids[0]) | (kid == q_ids[1]) | (kid == q_ids[2]) | (kid == q_ids[3])
                live[0, many * GROUP + n] = (head * slots + k_slot) * BLOCKS + j
                live[1, many * GROUP + n] = kid
                n = n + hit.astype(jnp.int32)
        for pad in range(GROUP - 1):
            live[0, many * GROUP + n + pad] = head * slots * BLOCKS
            live[1, many * GROUP + n + pad] = -1
        rest = lax.rem(n, GROUP)
        groups = n // GROUP + (rest == GROUP - 1).astype(jnp.int32)
        small = ((rest == 1) | (rest == 2)).astype(jnp.int32)
        for g in range(SIDE):
            live[4, many + g] = flat
        live[5, pair] = flat
        many = many + groups
        for j in range(GROUP // 2):
            live[2, pair * (GROUP // 2) + j] = live[0, many * GROUP + j]
            live[3, pair * (GROUP // 2) + j] = live[1, many * GROUP + j]
        pair = pair + small

    def unit(size, parts, row, g, carry):
        flat = live[4 + row // 2, g]
        query = qd[flat, :, 0:HD]
        grad = qd[flat, :, HD:2 * HD]
        lse = rows[flat, 0:1, :]
        delta = rows[flat, 1:2, :]
        ids_row = rows[flat, 2:3, :].astype(jnp.int32)
        spans = []
        kids = []
        for j in range(size):
            at = live[row, g * size + j]
            spans.append(pl.ds(pl.multiple_of(at * BLOCK, BLOCK), BLOCK))
            kids.append(live[row + 1, g * size + j])
        key = jnp.concatenate([ks[p, :] for p in spans], axis=0)
        value = jnp.concatenate([vs[p, :] for p in spans], axis=0)
        wide = FRAMES // parts
        cuts = [slice(c * wide, (c + 1) * wide) for c in range(parts)]
        fronts = [(dot(key, query[c], NT), dot(value, grad[c], NT)) for c in cuts]
        add_v = add_k = None
        for c, (scores, dprob) in zip(cuts, fronts):
            probs = []
            dscores = []
            for j in range(size):
                cut = slice(j * BLOCK, (j + 1) * BLOCK)
                prob = jnp.exp2(scores[cut] * F32(SCALE * LOG2E) - lse[:, c])
                prob = jnp.where(ids_row[:, c] == kids[j], prob, F32(0.0))
                probs.append(prob.astype(BF16))
                dscores.append((prob * (dprob[cut] - delta[:, c])).astype(BF16))
            prob_b = jnp.concatenate(probs, axis=0)
            dscore = jnp.concatenate(dscores, axis=0)
            part_v = dot(prob_b, grad[c], NN)
            part_k = dot(dscore, query[c], NN)
            add_v = part_v if add_v is None else add_v + part_v
            add_k = part_k if add_k is None else add_k + part_k
            dq_t[flat, :, c] += dot(key, dscore, TN)
        for j in range(size):
            cut = slice(j * BLOCK, (j + 1) * BLOCK)
            dv[spans[j], :] += add_v[cut]
            dk[spans[j], :] += add_k[cut]
        return carry

    lax.fori_loop(0, many, functools.partial(unit, GROUP, 2, 0), 0)
    lax.fori_loop(0, pair, functools.partial(unit, GROUP // 2, 1, 2), 0)


def resume(before, slots, old_k, old_v, old_q, dk, dv, dq_t):
    done = before * FRAMES
    for head in range(2):
        first, last = head * slots * FRAMES, (head + 1) * slots * FRAMES
        for new, old in ((dk, old_k), (dv, old_v)):
            new[first:first + done, :] = old[head * done:(head + 1) * done, :]
            new[first + done:last, :] = jnp.zeros((last - first - done, HD), F32)
        dq_t[head * slots:head * slots + before] = old_q[head * before:(head + 1) * before]
        dq_t[head * slots + before:(head + 1) * slots] = jnp.zeros((slots - before, HD, FRAMES), F32)


def own_kernel(px, py, hx, hy, dk, dv, dq_t, *scratch):
    qd, ks, vs, extras, rows, ids_v, ids_s, live, sem, id_sem, hold_sem = scratch
    top = pl.ds(0, FRAMES + EXTRA)
    holds = fetch([(px.at[top], hx), (py.at[top], hy)], hold_sem)
    copies, to_scalars = load_chunks(1, (px,), (py,), qd, ks, vs, extras, rows, ids_v, ids_s, sem, id_sem)
    dk[...] = jnp.zeros_like(dk)
    dv[...] = jnp.zeros_like(dv)
    dq_t[...] = jnp.zeros_like(dq_t)
    to_scalars.wait()
    for i, copy in enumerate(copies):
        if i % 4:
            copy.wait()
    pairs = [(head, 0, (0,)) for head in range(2)]
    run_pairs(pairs, 1, qd, ks, vs, rows, ids_s, live, dk, dv, dq_t)
    for copy in holds:
        copy.wait()


def early_kernel(*refs):
    xs, ys = refs[0:EARLY], refs[EARLY:2 * EARLY]
    old_k, old_v, old_q = refs[2 * EARLY:2 * EARLY + 3]
    dk, dv, dq_t = refs[2 * EARLY + 3:2 * EARLY + 6]
    qd, ks, vs, extras, rows, ids_v, ids_s, live, sem, id_sem = refs[2 * EARLY + 6:]
    copies, to_scalars = load_chunks(EARLY, xs, ys, qd, ks, vs, extras, rows, ids_v, ids_s, sem, id_sem)
    resume(1, EARLY, old_k, old_v, old_q, dk, dv, dq_t)
    to_scalars.wait()
    for i, copy in enumerate(copies):
        if i % 4:
            copy.wait()
    pairs = [(head, s, range(1, EARLY) if s == 0 else range(EARLY)) for s in range(EARLY) for head in range(2)]
    run_pairs(pairs, EARLY, qd, ks, vs, rows, ids_s, live, dk, dv, dq_t)


def late_kernel(*refs):
    xs, ys = refs[0:4], refs[4:8]
    old_k, old_v, old_q = refs[8:11]
    gw_own = refs[11]
    ox, oy = refs[12:16], refs[16:20]
    dk, dv, dq_t, gw_in, gw_sum, gw_sem, qd, ks, vs, extras, rows, ids_v, ids_s, live, sem, id_sem = refs[20:]
    low = pl.ds(FRAMES + EXTRA, GW_IN)
    gw_copies = fetch([(part.at[low], gw_in.at[n]) for n, part in enumerate(ys[1:])], gw_sem)
    copies, to_scalars = load_chunks(SIDE, xs, ys, qd, ks, vs, extras, rows, ids_v, ids_s, sem, id_sem)
    resume(EARLY, SIDE, old_k, old_v, old_q, dk, dv, dq_t)
    finish(gw_copies)
    total = gw_own[...]
    for n in range(SIDE - 1):
        total = total + gw_in[n].astype(F32)
    gw_sum[...] = total
    for s in range(SIDE):
        at = lax.rem(lax.axis_index("ctx") + SIDE - OFFSETS[s], SIDE) * HD
        cut = pl.ds(pl.multiple_of(at, HD), HD)
        for half in range(2):
            piece = gw_sum[half * GW:(half + 1) * GW, cut].astype(ox[s].dtype)
            ox[s][FRAMES:, half * HD:(half + 1) * HD] = piece[0:GW_OUT]
            at_rest = FRAMES + half * GW_REST
            ox[s][at_rest:at_rest + GW_REST, 2 * HD:] = piece[GW_OUT:]
        ox[s][FRAMES + 2 * GW_REST:, 2 * HD:] = jnp.zeros((GW_OUT - 2 * GW_REST, HD), ox[s].dtype)
    to_scalars.wait()
    for i, copy in enumerate(copies):
        if i % 4:
            copy.wait()
    pairs = [
        (head, s, range(EARLY, SIDE) if s < EARLY else range(SIDE)) for s in range(SIDE) for head in range(2)
    ]
    run_pairs(pairs, SIDE, qd, ks, vs, rows, ids_s, live, dk, dv, dq_t)
    for s in range(SIDE):
        for head, out_q, out_k in ((0, ox[s], oy[s]), (1, oy[s], ox[s])):
            flat = head * SIDE + s
            span = pl.ds(flat * FRAMES, FRAMES)
            out_q[:FRAMES, 0:HD] = (dq_t[flat].T * F32(SCALE)).astype(out_q.dtype)
            out_k[:FRAMES, HD:2 * HD] = (dk[span, :] * F32(SCALE)).astype(out_k.dtype)
            out_k[:FRAMES, 2 * HD:3 * HD] = dv[span, :].astype(out_k.dtype)


def chunk_scratch(slots):
    return [
        pltpu.VMEM((2 * slots, FRAMES, 2 * HD), BF16),
        pltpu.VMEM((2 * slots * FRAMES, HD), BF16),
        pltpu.VMEM((2 * slots * FRAMES, HD), BF16),
        pltpu.VMEM((2 * slots, EXTRA, FRAMES), BF16),
        pltpu.VMEM((2 * slots, 8, FRAMES), F32),
        pltpu.VMEM((2 * SIDE, FRAMES), jnp.int32),
        pltpu.SMEM((2 * SIDE, FRAMES), jnp.int32),
        pltpu.SMEM((6, LISTED), jnp.int32),
        pltpu.SemaphoreType.DMA((2 * slots, 4)),
        pltpu.SemaphoreType.DMA,
    ]


def own_tiles(px, py):
    held = jax.ShapeDtypeStruct((FRAMES + EXTRA, 4 * HD), BF16)
    kv = jax.ShapeDtypeStruct((2 * FRAMES, HD), F32)
    q = jax.ShapeDtypeStruct((2, HD, FRAMES), F32)
    out = pl.pallas_call(
        own_kernel,
        out_shape=(held, held, kv, kv, q),
        in_specs=[ANY] * 2,
        out_specs=(VMEM,) * 5,
        scratch_shapes=chunk_scratch(1) + [pltpu.SemaphoreType.DMA((2,))],
        compiler_params=pltpu.CompilerParams(vmem_limit_bytes=40 * MIB),
        cost_estimate=pl.CostEstimate(flops=700_000_000, bytes_accessed=4_000_000, transcendentals=500_000),
    )(px, py)
    return out[0:2], out[2:5]


def early_tiles(xs, ys, partial):
    kv = jax.ShapeDtypeStruct((2 * EARLY * FRAMES, HD), F32)
    q = jax.ShapeDtypeStruct((2 * EARLY, HD, FRAMES), F32)
    return pl.pallas_call(
        early_kernel,
        out_shape=(kv, kv, q),
        in_specs=[ANY] * (2 * EARLY) + [VMEM] * 3,
        out_specs=(VMEM,) * 3,
        scratch_shapes=chunk_scratch(EARLY),
        compiler_params=pltpu.CompilerParams(vmem_limit_bytes=40 * MIB),
        cost_estimate=pl.CostEstimate(flops=5_000_000_000, bytes_accessed=8_000_000, transcendentals=2_000_000),
    )(*xs, *ys, *partial)


def late_tiles(xs, ys, partial, gw):
    shapes = [
        jax.ShapeDtypeStruct((rows, 3 * HD), F32 if s == 0 else BF16) for rows in (FRAMES + GW_OUT, FRAMES) for s in range(SIDE)
    ]
    acc = pltpu.VMEM((2 * SIDE * FRAMES, HD), F32)
    out = pl.pallas_call(
        late_kernel,
        out_shape=tuple(shapes),
        in_specs=[ANY] * 8 + [VMEM] * 4,
        out_specs=(VMEM,) * 8,
        scratch_shapes=[
            acc,
            acc,
            pltpu.VMEM((2 * SIDE, HD, FRAMES), F32),
            pltpu.VMEM((SIDE - 1, GW_IN, 4 * HD), BF16),
            pltpu.VMEM((GW_IN, 4 * HD), F32),
            pltpu.SemaphoreType.DMA((SIDE - 1,)),
        ]
        + chunk_scratch(SIDE),
        compiler_params=pltpu.CompilerParams(vmem_limit_bytes=40 * MIB),
        cost_estimate=pl.CostEstimate(flops=5_000_000_000, bytes_accessed=8_000_000, transcendentals=2_000_000),
    )(*xs, *ys, *partial, gw)
    return out[0:4], out[4:8]


def merge_kernel(*refs):
    xs, ys = refs[0:4], refs[4:8]
    q_ref, k_ref, v_ref, w_ref = refs[8:12]
    for out, column, first in ((q_ref, 0, 0), (k_ref, 1, 1), (v_ref, 2, 1)):
        for head in range(2):
            parts = xs if head == first else ys
            cut = slice(column * HD, (column + 1) * HD)
            total = parts[0][:FRAMES, cut]
            for part in parts[1:]:
                total = total + part[:FRAMES, cut].astype(F32)
            out[:, head * HD:(head + 1) * HD] = total.astype(BF16)
    total = xs[0][FRAMES:, :]
    for part in xs[1:]:
        total = total + part[FRAMES:, :].astype(F32)
    w_ref[0:GW_OUT, :] = total[:, 0:2 * HD]
    for half in range(2):
        w_ref[GW_OUT:, half * HD:(half + 1) * HD] = total[half * GW_REST:(half + 1) * GW_REST, 2 * HD:]


def merge(xs, ys):
    shape = jax.ShapeDtypeStruct((FRAMES, 2 * HD), BF16)
    return pl.pallas_call(
        merge_kernel,
        out_shape=(shape, shape, shape, jax.ShapeDtypeStruct((GW, 2 * HD), F32)),
        compiler_params=pltpu.CompilerParams(vmem_limit_bytes=32 * MIB),
        cost_estimate=pl.CostEstimate(flops=2_000_000, bytes_accessed=4_000_000, transcendentals=0),
    )(*xs, *ys)


def shards(queries, keys, values, attn_out, lse, out_grad, w_out, block_utt):
    own, px, py = pack(queries, keys, values, attn_out, lse, out_grad, w_out, block_utt)
    near = [along_x(px, 1), along_y(py[0], 1), along_x(px, 3), along_y(py[1], 3)]
    held, partial = own_tiles(px, py[2])
    far_x, held, near[0], near[2] = lax.optimization_barrier((px, held, near[0], near[2]))
    far_y, partial, near[1], near[3] = lax.optimization_barrier((py[2], partial, near[1], near[3]))
    xs = [held[0], near[0], near[2], along_x(far_x, 2)]
    ys = [held[1], near[1], near[3], along_y(far_y, 2)]
    partial = early_tiles(xs[:EARLY], ys[:EARLY], partial)
    ox, oy = late_tiles(xs, ys, partial, own)
    bx, by = [ox[0]], [oy[0]]
    for s in (3, 1, 2):
        bx.append(along_x(ox[s], SIDE - OFFSETS[s]))
        by.append(along_y(oy[s], SIDE - OFFSETS[s]))
    return merge(bx, by)


def solution(mesh):
    return jax.shard_map(
        shards,
        mesh=mesh,
        in_specs=(
            P(("dp", "ctx"), "head"),
            P(("dp", "ctx"), "head"),
            P(("dp", "ctx"), "head"),
            P(("dp", "ctx"), "head"),
            P("head", ("dp", "ctx")),
            P(("dp", "ctx"), None),
            P("head", None),
            P(("dp", "ctx")),
        ),
        out_specs=(
            P(("dp", "ctx"), "head"),
            P(("dp", "ctx"), "head"),
            P(("dp", "ctx"), "head"),
            P("ctx", ("dp", "head")),
        ),
        check_vma=False,
    )
```
